32 devices in a mesh: ctx: 4 (over z), head: 2 (over x), dp: 4 (over y, core).
Axes of the slice: x: 2, y: 2, z: 4, core: 2. Of those that a mesh axis runs over, the one named last changes fastest.
Arguments:
- queries: bfloat16 [2048, 4096], P(('dp', 'ctx'), 'head'), parts along dimension 0, may hold values from -6 to 6
- key_rows: bfloat16 [2048, 4096], P(('dp', 'ctx'), 'head'), parts along dimension 0, may hold values from -6 to 6
- value_rows: bfloat16 [2048, 4096], P(('dp', 'ctx'), 'head'), parts along dimension 0, may hold values from -6 to 6
- gate_values: bfloat16 [2048, 4096], P(('dp', 'ctx'), 'head'), parts along dimension 0, may hold values from -6 to 6
- cotangent: bfloat16 [2048, 4096], P(('dp', 'ctx'), 'head'), parts along dimension 0, may hold values from -6 to 6
- decay_rates: float32 [16, 4096], P(None, 'head'), may hold values from 0 to 1, as said below
- residues: float32 [16, 4096], P(None, 'head'), may hold values from -4 to 4
- skip_gain: float32 [4096], P('head'), may hold values from -6 to 6
Outputs:
- queries_adjoint: bfloat16 [2048, 4096], P(('dp', 'ctx'), 'head'), parts along dimension 0
- keys_adjoint: bfloat16 [2048, 4096], P(('dp', 'ctx'), 'head'), parts along dimension 0
- values_adjoint: bfloat16 [2048, 4096], P(('dp', 'ctx'), 'head'), parts along dimension 0
- gate_adjoint: bfloat16 [2048, 4096], P(('dp', 'ctx'), 'head'), parts along dimension 0
- residues_adjoint: float32 [64, 4096], P('dp', 'head'), parts along dimension 0
The draws below stay inside these ranges and needn't reach their ends.
There are 4 independent parts, one for each index of `dp`. The reference program is written for one: setup_inputs(seed, part) draws one part's arguments, and reference() takes and returns one part's arrays. A program takes and returns all parts, laid end to end along the dimension named above; an argument that names none is the same for every part. Nothing has to cross between parts.
Inputs may be any that keep to these rules, and one draw needn't show every extreme that they name: `decay_rates`: every rate lies between 0.6 / 512 and 1/16 per position.
All inputs are finite; a program needn't handle non-finite values.
Results may differ from the reference program's by a relative error of at most 0.0094.
Values may be sent and summed in bfloat16 or wider, within the bound.
A program may use at most 128 MiB of HBM per device.

```python
import math
import jax
import jax.numpy as jnp
from jax import lax

HEADS = 32
HEAD = 128
POLES = 16
TOK_DEV = 128
WIN = 4
TOKENS = 512
CH = 4096
N_CTX = 4


def paired_draw(key):
    base_key = jax.random.fold_in(key, 4242)
    query_key, other_key = jax.random.split(base_key, 2)
    shape_pair = (TOKENS, HEADS * HEAD)
    query_part = jnp.clip(2.5 * jax.random.normal(query_key, shape_pair, jnp.float32), -6.0, 6.0)
    key_part = jnp.clip(jax.random.normal(other_key, shape_pair, jnp.float32), -6.0, 6.0)
    return (query_part, key_part)


def draw_queries(key, part):
    return paired_draw(key)[0].astype(jnp.bfloat16)


def draw_key_rows(key, part):
    return paired_draw(key)[1].astype(jnp.bfloat16)


def draw_decay_rates(key, part):
    pick_key, slow_key, fast_key = jax.random.split(jax.random.fold_in(key, 99), 3)
    shape_rates = (POLES, HEADS * HEAD)
    slow_share = 0.5
    slow_low = math.log(0.6 / TOKENS)
    slow_high = math.log(2.3 / TOKENS)
    fast_low = math.log(1.0 / 64.0)
    fast_high = math.log(1.0 / 16.0)
    slow_rates = jnp.exp(slow_low + jax.random.uniform(slow_key, shape_rates, jnp.float32) * (slow_high - slow_low))
    fast_rates = jnp.exp(fast_low + jax.random.uniform(fast_key, shape_rates, jnp.float32) * (fast_high - fast_low))
    picked = jax.random.uniform(pick_key, shape_rates, jnp.float32) < slow_share
    return jnp.where(picked, slow_rates, fast_rates).astype(jnp.float32)


def levels(key, extent, cuts, least, top_value):
    def one(position, parts):
        heights = jax.random.uniform(jax.random.fold_in(jax.random.fold_in(key, 6), position), (parts,), jnp.float32, least / len(cuts), top_value / len(cuts))
        return jnp.repeat(jnp.exp(heights), extent[position] // parts).reshape((-1,) + (1,) * (len(extent) - position - 1))

    gain = one(*cuts[0])
    for cut in cuts[1:]:
        gain = gain * one(*cut)
    return gain


def gaussian(own_key, dims, width, limit, shards=(), held_as=jnp.bfloat16):
    values = width * jax.random.normal(own_key, dims, jnp.float32)
    if shards:
        values = values * levels(own_key, dims, shards, -0.22, 0.18)
    return jnp.clip(values, -limit, limit).astype(held_as)


def setup_inputs(seed: int = 0, part: int = 0) -> dict:
    splits = jax.random.split(jax.random.key(seed), 9)
    own_keys = jax.random.split(jax.random.fold_in(splits[8], part), 9)
    return {
        "queries": draw_queries(jax.random.fold_in(jax.random.fold_in(splits[8], part), 71), part),
        "key_rows": draw_key_rows(jax.random.fold_in(jax.random.fold_in(splits[8], part), 71), part),
        "value_rows": gaussian(own_keys[2], (TOKENS, CH), 1.0, 6.0, ((0, 4), (1, 2))),
        "gate_values": gaussian(own_keys[3], (TOKENS, CH), 1.0, 6.0, ((0, 4), (1, 2))),
        "cotangent": gaussian(own_keys[4], (TOKENS, CH), 1.0, 6.0, ((0, 4), (1, 2))),
        "decay_rates": draw_decay_rates(jax.random.fold_in(splits[8], 71), part),
        "residues": gaussian(splits[6], (POLES, CH), 0.25, 4.0, ((1, 2),), jnp.float32),
        "skip_gain": gaussian(splits[7], (CH,), 1.0, 6.0, ((0, 2),), jnp.float32),
    }


def to_half(array):
    return lax.optimization_barrier(array.astype(jnp.bfloat16)).astype(jnp.float32)

def window_mask(row_count):
    row_ids = jnp.arange(row_count)[:, None, None]
    lag_ids = jnp.arange(WIN + 1)[None, :, None]
    column_ids = jnp.arange(row_count)[None, None, :]
    return ((lag_ids > 0) | (column_ids <= row_ids)) & ((lag_ids < WIN) | (column_ids > row_ids))

def modal_pass(signal, damping, opening, mixing, skip_gain, partner, weights):
    piece_rows = min(128, TOK_DEV)
    pieces = TOKENS // piece_rows
    offsets = jnp.arange(piece_rows, dtype=jnp.float32)[:, None, None]
    growth = jnp.exp(damping[None] * offsets)
    shrink = jnp.exp(-damping[None] * offsets)
    entering = jnp.exp(-damping[None] * (offsets + 1.0))

    def advance(carried, head_item):
        segment, matched = head_item
        local_part = shrink * jnp.cumsum(growth * segment[:, None, :], axis=0)
        states = local_part + entering * carried[None]
        mixture = lax.optimization_barrier(jnp.sum(mixing[None] * states, axis=1)) + skip_gain[None] * segment
        product = lax.optimization_barrier(jnp.sum(weights[None] * matched[:, None, :] * states, axis=0))
        return (states[-1], (mixture, product))
    closing, (mixture, product) = lax.scan(advance, opening, (signal.reshape(pieces, piece_rows, -1), partner.reshape(pieces, piece_rows, -1)))
    return (closing, mixture.reshape(TOKENS, -1), lax.optimization_barrier(jnp.sum(product, axis=0)))

def periodic_pass(signal, damping, mixing, skip_gain, partner, weights):
    zero_state = jnp.zeros(damping.shape, jnp.float32)
    closing, unused_mix, unused_sum = modal_pass(signal, damping, zero_state, mixing, skip_gain, partner, weights)
    loop_gap = -jnp.expm1(-damping * TOKENS)
    closing_again, mixture, product = modal_pass(signal, damping, closing / loop_gap, mixing, skip_gain, partner, weights)
    return (mixture, product)

def head_pass(head_item):
    query_head, key_head, value_head, adjoint_head = [member.astype(jnp.float32) for member in head_item]
    key_window = jnp.stack([jnp.roll(key_head, lag_block, axis=0) for lag_block in range(WIN + 1)])
    value_window = jnp.stack([jnp.roll(value_head, lag_block, axis=0) for lag_block in range(WIN + 1)])
    scale_factor = 1.0 / math.sqrt(HEAD)
    scores = jnp.einsum('nre,knse->nrks', query_head, key_window) * scale_factor
    allowed = window_mask(TOK_DEV)[None]
    masked = jnp.where(allowed, scores, -jnp.inf)
    row_top = lax.optimization_barrier(jnp.max(masked, axis=(2, 3), keepdims=True))
    raised = jnp.exp(masked - row_top)
    probability = raised / lax.optimization_barrier(jnp.sum(raised, axis=(2, 3), keepdims=True))
    rounded_prob = to_half(probability)
    attended = jnp.einsum('nrks,knse->nre', rounded_prob, value_window).astype(jnp.bfloat16)
    weight_adjoint = jnp.einsum('nre,knse->nrks', adjoint_head, value_window)
    inner_sum = lax.optimization_barrier(jnp.sum(probability * weight_adjoint, axis=(2, 3), keepdims=True))
    score_adjoint = to_half(probability * (weight_adjoint - inner_sum) * scale_factor)
    query_adjoint = jnp.einsum('nrks,knse->nre', score_adjoint, key_window).astype(jnp.bfloat16)
    key_parts = to_half(jnp.einsum('nrks,nre->knse', score_adjoint, query_head))
    value_parts = to_half(jnp.einsum('nrks,nre->knse', rounded_prob, adjoint_head))
    key_total = sum((jnp.roll(key_parts[lag_block], -lag_block, axis=0) for lag_block in range(WIN + 1)))
    value_total = sum((jnp.roll(value_parts[lag_block], -lag_block, axis=0) for lag_block in range(WIN + 1)))
    return (attended, query_adjoint, key_total.astype(jnp.bfloat16), value_total.astype(jnp.bfloat16))

def split_heads(array):
    return array.reshape(N_CTX, TOK_DEV, HEADS, HEAD).transpose(2, 0, 1, 3)

def merge_heads(array):
    return array.transpose(1, 2, 0, 3).reshape(TOKENS, HEADS * HEAD)

def reference(queries, key_rows, value_rows, gate_values, cotangent, decay_rates, residues, skip_gain):
    damping = decay_rates
    weights = jnp.sqrt(-jnp.expm1(-2.0 * damping))
    mixing = residues * weights
    delta_rows = cotangent.astype(jnp.float32) * gate_values.astype(jnp.float32)
    no_partner = jnp.zeros_like(delta_rows)
    reversed_mix, unused_sum = periodic_pass(delta_rows[::-1], damping, mixing, skip_gain, no_partner, weights)
    attended_adjoint = reversed_mix[::-1].astype(jnp.bfloat16)
    attended, query_adjoint, key_adjoint, value_adjoint = lax.map(head_pass, (split_heads(queries), split_heads(key_rows), split_heads(value_rows), split_heads(attended_adjoint)))
    mixture, residue_sum = periodic_pass(merge_heads(attended).astype(jnp.float32), damping, mixing, skip_gain, delta_rows, weights)
    gate_adjoint = (cotangent.astype(jnp.float32) * mixture).astype(jnp.bfloat16)
    return (merge_heads(query_adjoint), merge_heads(key_adjoint), merge_heads(value_adjoint), gate_adjoint, residue_sum)
```

```python
import functools
import math

import jax
import jax.numpy as jnp
from jax import lax
from jax.experimental import pallas as pl
from jax.experimental.pallas import tpu as pltpu
from jax.sharding import PartitionSpec as P

HEAD = 128
WIN = 4
SEGS = 8
POLE_GROUP = 8
MESH = pl.DeviceIdType.MESH


def decay_gap(x):
    inner = 1.0 - x * (1.0 / 7.0)
    for order in (6.0, 5.0, 4.0, 3.0, 2.0):
        inner = 1.0 - x * (1.0 / order) * inner
    return x * inner


def row_of(ref, kind, pole):
    return jnp.broadcast_to(ref[kind, pl.ds(pole, 1), :], (SEGS, HEAD))


def periodic_start(ends, par_ref, pole, backward):
    total = ends
    for power, kind in ((1, 3), (2, 4), (4, 5)):
        shift = SEGS - power if backward else power
        total = total + row_of(par_ref, kind, pole) * pltpu.roll(total, shift, 0)
    total = total * row_of(par_ref, 6, pole)
    return pltpu.roll(total, SEGS - 1 if backward else 1, 0)


def segment_ends(x_ref, par_ref, poles, steps, backward, unroll=4):
    lams = [row_of(par_ref, 0, pole) for pole in range(poles)]

    def body(index, states):
        for sub in range(unroll):
            step = index * unroll + sub
            if backward:
                step = steps - 1 - step
            x = x_ref[pl.ds(step, SEGS, stride=steps), :]
            states = tuple(lam * state + x for lam, state in zip(lams, states))
        return states

    zeros = tuple(jnp.zeros((SEGS, HEAD), jnp.float32) for _ in range(poles))
    ends = lax.fori_loop(0, steps // unroll, body, zeros)
    return [periodic_start(end, par_ref, pole, backward) for pole, end in enumerate(ends)]


def tree_sum(terms):
    terms = list(terms)
    while len(terms) > 1:
        paired = [a + b for a, b in zip(terms[::2], terms[1::2])]
        if len(terms) % 2:
            paired.append(terms[-1])
        terms = paired
    return terms[0]


def fast_kernel(
    members, local_heads,
    q_ref, k_ref, v_ref, gate_ref, cot_ref, decay_ref, residue_ref, skip_ref,
    dq_ref, dk_ref, dv_ref, dgate_ref, dres_ref,
    stage, inbox, outbox, landed, res_box, res_landed,
    par_ref, delta_ref, y_ref, att_ref, da_ref, dk_acc, dv_acc,
    in_send, in_recv, grad_send, grad_recv, mix_send, mix_recv, res_send, res_recv,
):
    me = lax.axis_index("ctx")
    rows = q_ref.shape[0]
    tokens = rows * members
    steps = tokens // SEGS
    poles = decay_ref.shape[0]
    group = local_heads // members
    scale = 1.0 / math.sqrt(HEAD)

    barrier = pltpu.get_barrier_semaphore()
    for off in range(1, members):
        pl.semaphore_signal(
            barrier, inc=1, device_id={"ctx": lax.rem(me + off, members)}, device_id_type=MESH
        )
    stage[0] = (cot_ref[...].astype(jnp.float32) * gate_ref[...].astype(jnp.float32)).astype(
        jnp.bfloat16
    )
    stage[1] = q_ref[...]
    stage[2] = k_ref[...]
    stage[3] = v_ref[...]
    pl.semaphore_wait(barrier, members - 1)

    def lanes(owner, head):
        return pl.ds(pl.multiple_of((owner * group + head) * HEAD, HEAD), HEAD)

    def rows_of(owner):
        return pl.ds(pl.multiple_of(owner * rows, rows), rows)

    def dest(off):
        return lax.rem(me + off, members)

    def source(off):
        return lax.rem(me + members - off, members)

    def remote(src, dst, send, recv, target):
        return pltpu.make_async_remote_copy(
            src_ref=src, dst_ref=dst, send_sem=send, recv_sem=recv,
            device_id={"ctx": target}, device_id_type=MESH,
        )

    def in_copy(head, off):
        return remote(
            stage.at[:, :, lanes(dest(off), head)], inbox.at[head, :, rows_of(me), :],
            in_send.at[head, off - 1], in_recv.at[head, off - 1], dest(off),
        )

    def in_arrival(head, off):
        return remote(
            stage.at[:, :, lanes(dest(off), head)], inbox.at[head, :, rows_of(source(off)), :],
            in_send.at[head, off - 1], in_recv.at[head, off - 1], dest(off),
        )

    def grad_copy(head, off, owner):
        return remote(
            outbox.at[head, pl.ds(0, 3), rows_of(dest(off)), :],
            landed.at[pl.ds(0, 3), :, lanes(owner, head)],
            grad_send.at[head, off - 1], grad_recv.at[head, off - 1], dest(off),
        )

    def mix_copy(head, off, owner):
        return remote(
            outbox.at[head, pl.ds(3, 1), rows_of(dest(off)), :],
            landed.at[pl.ds(3, 1), :, lanes(owner, head)],
            mix_send.at[head, off - 1], mix_recv.at[head, off - 1], dest(off),
        )

    def res_copy(head, off, owner):
        return remote(
            res_box.at[head], res_landed.at[:, lanes(owner, head)],
            res_send.at[head, off - 1], res_recv.at[head, off - 1], dest(off),
        )

    def send_inputs(head, carry):
        for off in range(1, members):
            in_copy(head, off).start()
        return carry

    lax.fori_loop(0, group, send_inputs, 0)

    def one_head(head, carry):
        mine = lanes(me, head)
        damping = decay_ref[:, mine]
        weights = jnp.sqrt(decay_gap(2.0 * damping))
        par_ref[0] = 1.0 - decay_gap(damping)
        par_ref[1] = residue_ref[:, mine] * weights
        par_ref[2] = weights
        par_ref[3] = jnp.exp(-damping * steps)
        par_ref[4] = jnp.exp(-damping * (2 * steps))
        par_ref[5] = jnp.exp(-damping * (4 * steps))
        par_ref[6] = 1.0 / (1.0 - jnp.exp(-damping * tokens))
        skip = jnp.broadcast_to(skip_ref[:, mine], (SEGS, HEAD))
        inbox[head, :, rows_of(me), :] = stage[:, :, mine]
        for off in range(1, members):
            in_arrival(head, off).wait_recv()
        delta_ref[...] = inbox[head, 0].astype(jnp.float32)

        entering = segment_ends(delta_ref, par_ref, poles, steps, True)
        lams = [row_of(par_ref, 0, pole) for pole in range(poles)]
        mixes = [row_of(par_ref, 1, pole) for pole in range(poles)]

        def backward_body(index, states):
            for sub in range(2):
                step = steps - 1 - (index * 2 + sub)
                x = delta_ref[pl.ds(step, SEGS, stride=steps), :]
                states = tuple(lam * state + x for lam, state in zip(lams, states))
                y_ref[pl.ds(step, SEGS, stride=steps), :] = skip * x + tree_sum(
                    mix * state for mix, state in zip(mixes, states)
                )
            return states

        lax.fori_loop(0, steps // 2, backward_body, tuple(entering))
        da_ref[...] = y_ref[...].astype(jnp.bfloat16)

        key_head = inbox[head, 2]
        value_head = inbox[head, 3]
        for block in range(members):
            span = pl.ds(block * rows, rows)
            query = inbox[head, 1, span, :]
            adjoint = da_ref[span, :]
            scores = lax.dot_general(
                query, key_head, (((1,), (1,)), ((), ())), preferred_element_type=jnp.float32
            ) * scale
            raised = jnp.exp(scores - jnp.max(scores, axis=1, keepdims=True))
            probability = raised * (1.0 / jnp.sum(raised, axis=1, keepdims=True))
            rounded = probability.astype(jnp.bfloat16)
            attended = jnp.dot(rounded, value_head, preferred_element_type=jnp.float32)
            att_ref[span, :] = attended.astype(jnp.bfloat16).astype(jnp.float32)
            weight_adjoint = lax.dot_general(
                adjoint, value_head, (((1,), (1,)), ((), ())), preferred_element_type=jnp.float32
            )
            inner = jnp.sum(probability * weight_adjoint, axis=1, keepdims=True)
            score_adjoint = (probability * (weight_adjoint - inner) * scale).astype(jnp.bfloat16)
            outbox[head, 0, span, :] = jnp.dot(
                score_adjoint, key_head, preferred_element_type=jnp.float32
            ).astype(jnp.bfloat16)
            key_part = lax.dot_general(
                score_adjoint, query, (((0,), (0,)), ((), ())), preferred_element_type=jnp.float32
            )
            value_part = lax.dot_general(
                rounded, adjoint, (((0,), (0,)), ((), ())), preferred_element_type=jnp.float32
            )
            if block == 0:
                dk_acc[...] = key_part
                dv_acc[...] = value_part
            else:
                dk_acc[...] += key_part
                dv_acc[...] += value_part
        outbox[head, 1] = dk_acc[...].astype(jnp.bfloat16)
        outbox[head, 2] = dv_acc[...].astype(jnp.bfloat16)
        for off in range(1, members):
            grad_copy(head, off, me).start()

        entering_forward = segment_ends(att_ref, par_ref, poles, steps, False)
        for first in range(0, poles, POLE_GROUP):
            chosen = range(first, first + POLE_GROUP)
            group_lams = [row_of(par_ref, 0, pole) for pole in chosen]
            group_mixes = [row_of(par_ref, 1, pole) for pole in chosen]

            def forward_body(index, item, first=first, lams=group_lams, mixes=group_mixes):
                states, sums = item
                for sub in range(2):
                    step = index * 2 + sub
                    here = pl.ds(step, SEGS, stride=steps)
                    x = att_ref[here, :]
                    delta = delta_ref[here, :]
                    states = tuple(lam * state + x for lam, state in zip(lams, states))
                    sums = tuple(total + delta * state for total, state in zip(sums, states))
                    base = skip * x if first == 0 else y_ref[here, :]
                    y_ref[here, :] = base + tree_sum(
                        mix * state for mix, state in zip(mixes, states)
                    )
                return states, sums

            zeros = tuple(jnp.zeros((SEGS, HEAD), jnp.float32) for _ in chosen)
            starts = tuple(entering_forward[pole] for pole in chosen)
            unused, sums = lax.fori_loop(0, steps // 2, forward_body, (starts, zeros))
            for pole, total in zip(chosen, sums):
                res_box[head, pl.ds(pole, 1), :] = (
                    jnp.sum(total, axis=0, keepdims=True) * par_ref[2, pl.ds(pole, 1), :]
                )
        outbox[head, 3] = y_ref[...].astype(jnp.bfloat16)
        for off in range(1, members):
            mix_copy(head, off, me).start()
            res_copy(head, off, me).start()
        landed[:, :, mine] = outbox[head, :, rows_of(me), :]
        res_landed[:, mine] = res_box[head]
        return carry

    lax.fori_loop(0, group, one_head, 0)

    def finish(head, carry):
        for off in range(1, members):
            grad_copy(head, off, source(off)).wait_recv()
            mix_copy(head, off, source(off)).wait_recv()
            res_copy(head, off, source(off)).wait_recv()
        return carry

    lax.fori_loop(0, group, finish, 0)
    dq_ref[...] = landed[0]
    dk_ref[...] = landed[1]
    dv_ref[...] = landed[2]
    dgate_ref[...] = (
        cot_ref[...].astype(jnp.float32) * landed[3].astype(jnp.float32)
    ).astype(jnp.bfloat16)
    dres_ref[...] = res_landed[...]

    def sent(head, carry):
        for off in range(1, members):
            in_copy(head, off).wait_send()
            grad_copy(head, off, me).wait_send()
            mix_copy(head, off, me).wait_send()
            res_copy(head, off, me).wait_send()
        return carry

    lax.fori_loop(0, group, sent, 0)


def fast_local(queries, key_rows, value_rows, gate_values, cotangent, decay_rates, residues, skip_gain):
    members = lax.axis_size("ctx")
    rows, channels = queries.shape
    local_heads = channels // HEAD
    group = local_heads // members
    tokens = rows * members
    poles = decay_rates.shape[0]
    vmem = pl.BlockSpec(memory_space=pltpu.VMEM)
    wide = jax.ShapeDtypeStruct((rows, channels), jnp.bfloat16)
    sems = pltpu.SemaphoreType.DMA((group, members - 1))
    return pl.pallas_call(
        functools.partial(fast_kernel, members, local_heads),
        out_shape=(wide, wide, wide, wide, jax.ShapeDtypeStruct((poles, channels), jnp.float32)),
        in_specs=[vmem] * 8,
        out_specs=(vmem,) * 5,
        scratch_shapes=[
            pltpu.VMEM((4, rows, channels), jnp.bfloat16),
            pltpu.VMEM((group, 4, tokens, HEAD), jnp.bfloat16),
            pltpu.VMEM((group, 4, tokens, HEAD), jnp.bfloat16),
            pltpu.VMEM((4, rows, channels), jnp.bfloat16),
            pltpu.VMEM((group, poles, HEAD), jnp.float32),
            pltpu.VMEM((poles, channels), jnp.float32),
            pltpu.VMEM((7, poles, HEAD), jnp.float32),
            pltpu.VMEM((tokens, HEAD), jnp.float32),
            pltpu.VMEM((tokens, HEAD), jnp.float32),
            pltpu.VMEM((tokens, HEAD), jnp.float32),
            pltpu.VMEM((tokens, HEAD), jnp.bfloat16),
            pltpu.VMEM((tokens, HEAD), jnp.float32),
            pltpu.VMEM((tokens, HEAD), jnp.float32),
        ] + [sems] * 8,
        compiler_params=pltpu.CompilerParams(
            collective_id=0, has_side_effects=True, vmem_limit_bytes=48 * 1024 * 1024
        ),
    )(queries, key_rows, value_rows, gate_values, cotangent, decay_rates, residues,
      skip_gain.reshape(1, channels))


def passed_along(array, axis, by):
    length = lax.axis_size(axis)
    return lax.ppermute(array, axis, [(i, (i + by) % length) for i in range(length)])


def window_mask(row_count):
    row_ids = jnp.arange(row_count)[:, None, None]
    lag_ids = jnp.arange(WIN + 1)[None, :, None]
    column_ids = jnp.arange(row_count)[None, None, :]
    return ((lag_ids > 0) | (column_ids <= row_ids)) & ((lag_ids < WIN) | (column_ids > row_ids))


def local(queries, key_rows, value_rows, gate_values, cotangent, decay_rates, residues, skip_gain):
    members = lax.axis_size("ctx")
    tok_rows, channels = queries.shape
    local_heads = channels // HEAD
    scale_factor = 1.0 / math.sqrt(HEAD)
    weights = jnp.sqrt(-jnp.expm1(-2.0 * decay_rates))
    mixing = residues * weights
    loop_gap = -jnp.expm1(-decay_rates * (tok_rows * members))
    device_decay = jnp.exp(-decay_rates * tok_rows)
    piece_rows = min(128, tok_rows)
    pieces = tok_rows // piece_rows
    offsets = jnp.arange(piece_rows, dtype=jnp.float32)[:, None, None]
    piece_index = jnp.arange(pieces, dtype=jnp.float32)[:, None, None]
    start_weights = jnp.exp(-decay_rates[None] * offsets)
    growth = jnp.exp(decay_rates[None] * offsets)
    delta_rows = cotangent.astype(jnp.float32) * gate_values.astype(jnp.float32)
    blocks_delta = delta_rows.reshape(pieces, piece_rows, channels)
    piece_starts = jnp.einsum(
        "qpc,mqc->mpc", start_weights, blocks_delta, precision=lax.Precision.HIGHEST
    )
    head_state = jnp.sum(
        jnp.exp(-decay_rates[None] * (piece_index * piece_rows)) * piece_starts, axis=0
    )

    def backward_turn(turn_index, moving):
        return passed_along(device_decay * moving + head_state, "ctx", -1)

    incoming = lax.fori_loop(0, members, backward_turn, jnp.zeros_like(head_state)) / loop_gap

    def backward_step(carried, segment):
        local_part = growth * lax.cumsum(start_weights * segment[:, None, :], axis=0, reverse=True)
        states = local_part + jnp.exp(-decay_rates[None] * (piece_rows - offsets)) * carried[None]
        mixture = jnp.sum(mixing[None] * states, axis=1) + skip_gain[None] * segment
        return (states[0], mixture)

    unused_state, adjoint_rows = lax.scan(backward_step, incoming, blocks_delta, reverse=True)
    attended_adjoint = adjoint_rows.reshape(tok_rows, channels).astype(jnp.bfloat16)
    key_value = jnp.stack([key_rows, value_rows])
    window = [key_value]
    moving = key_value
    for lag_index in range(WIN):
        moving = passed_along(moving, "ctx", 1)
        window.append(moving)
    stacked = jnp.stack(window)
    key_window = stacked[:, 0]
    value_window = stacked[:, 1]
    allowed = window_mask(tok_rows)
    attended_parts = []
    query_adjoints = []
    key_partials = []
    value_partials = []
    for head_index in range(local_heads):
        first = head_index * HEAD
        query_head = queries[:, first : first + HEAD]
        key_head = key_window[:, :, first : first + HEAD]
        value_head = value_window[:, :, first : first + HEAD]
        adjoint_head = attended_adjoint[:, first : first + HEAD]
        scores = (
            jnp.einsum("re,kse->rks", query_head, key_head, preferred_element_type=jnp.float32)
            * scale_factor
        )
        masked = jnp.where(allowed, scores, -jnp.inf)
        row_top = jnp.max(masked, axis=(1, 2), keepdims=True)
        raised = jnp.exp(masked - row_top)
        probability = raised / jnp.sum(raised, axis=(1, 2), keepdims=True)
        rounded_prob = probability.astype(jnp.bfloat16)
        attended_parts.append(
            jnp.einsum(
                "rks,kse->re", rounded_prob, value_head, preferred_element_type=jnp.float32
            ).astype(jnp.bfloat16)
        )
        weight_adjoint = jnp.einsum(
            "re,kse->rks", adjoint_head, value_head, preferred_element_type=jnp.float32
        )
        inner_sum = jnp.sum(probability * weight_adjoint, axis=(1, 2), keepdims=True)
        score_adjoint = (probability * (weight_adjoint - inner_sum) * scale_factor).astype(
            jnp.bfloat16
        )
        query_adjoints.append(
            jnp.einsum(
                "rks,kse->re", score_adjoint, key_head, preferred_element_type=jnp.float32
            ).astype(jnp.bfloat16)
        )
        key_partials.append(
            jnp.einsum(
                "rks,re->kse", score_adjoint, query_head, preferred_element_type=jnp.float32
            ).astype(jnp.bfloat16)
        )
        value_partials.append(
            jnp.einsum(
                "rks,re->kse", rounded_prob, adjoint_head, preferred_element_type=jnp.float32
            ).astype(jnp.bfloat16)
        )
    attended = jnp.concatenate(attended_parts, axis=1)
    queries_adjoint = jnp.concatenate(query_adjoints, axis=1)
    partials = jnp.stack(
        [jnp.concatenate(key_partials, axis=2), jnp.concatenate(value_partials, axis=2)], axis=1
    )
    collected = partials[0].astype(jnp.float32)
    for lag_index in range(1, WIN + 1):
        collected = collected + passed_along(partials[lag_index], "ctx", -lag_index).astype(
            jnp.float32
        )
    keys_adjoint = collected[0].astype(jnp.bfloat16)
    values_adjoint = collected[1].astype(jnp.bfloat16)
    signal = attended.astype(jnp.float32)
    blocks_signal = signal.reshape(pieces, piece_rows, channels)
    end_weights = jnp.exp(-decay_rates[None] * (piece_rows - 1.0 - offsets))
    piece_ends = jnp.einsum(
        "qpc,mqc->mpc", end_weights, blocks_signal, precision=lax.Precision.HIGHEST
    )
    tail_state = jnp.sum(
        jnp.exp(-decay_rates[None] * ((pieces - 1.0 - piece_index) * piece_rows)) * piece_ends,
        axis=0,
    )

    def forward_turn(turn_index, moving):
        return passed_along(device_decay * moving + tail_state, "ctx", 1)

    arriving = lax.fori_loop(0, members, forward_turn, jnp.zeros_like(tail_state)) / loop_gap
    entering = jnp.exp(-decay_rates[None] * (offsets + 1.0))

    def forward_step(carried, step_item):
        segment, matched = step_item
        local_part = start_weights * jnp.cumsum(growth * segment[:, None, :], axis=0)
        states = local_part + entering * carried[None]
        mixture = jnp.sum(mixing[None] * states, axis=1) + skip_gain[None] * segment
        product = jnp.sum(weights[None] * matched[:, None, :] * states, axis=0)
        return (states[-1], (mixture, product))

    closing, (mixed_rows, products) = lax.scan(
        forward_step, arriving, (blocks_signal, blocks_delta)
    )
    gate_adjoint = (cotangent.astype(jnp.float32) * mixed_rows.reshape(tok_rows, channels)).astype(
        jnp.bfloat16
    )
    residues_adjoint = lax.psum(jnp.sum(products, axis=0), "ctx")
    return (queries_adjoint, keys_adjoint, values_adjoint, gate_adjoint, residues_adjoint)


def solution(mesh):
    in_specs = (
        P(("dp", "ctx"), "head"),
        P(("dp", "ctx"), "head"),
        P(("dp", "ctx"), "head"),
        P(("dp", "ctx"), "head"),
        P(("dp", "ctx"), "head"),
        P(None, "head"),
        P(None, "head"),
        P("head"),
    )
    out_specs = (
        P(("dp", "ctx"), "head"),
        P(("dp", "ctx"), "head"),
        P(("dp", "ctx"), "head"),
        P(("dp", "ctx"), "head"),
        P("dp", "head"),
    )
    members = mesh.shape["ctx"]

    def chosen(*arrays):
        rows, channels = arrays[0].shape
        whole = members == WIN and rows % 128 == 0 and (channels // HEAD) % members == 0
        return (fast_local if whole and arrays[5].shape[0] % POLE_GROUP == 0 else local)(*arrays)

    return jax.shard_map(chosen, mesh=mesh, in_specs=in_specs, out_specs=out_specs, check_vma=False)
```

```python
import functools
import math

import jax
import jax.numpy as jnp
from jax import lax
from jax.experimental import pallas as pl
from jax.experimental.pallas import tpu as pltpu
from jax.sharding import PartitionSpec as P

HEAD = 128
WIN = 4
SEGS = 8
POLE_GROUP = 8
MESH = pl.DeviceIdType.MESH


def decay_gap(x):
    inner = 1.0 - x * (1.0 / 7.0)
    for order in (6.0, 5.0, 4.0, 3.0, 2.0):
        inner = 1.0 - x * (1.0 / order) * inner
    return x * inner


def row_of(ref, kind, pole):
    return jnp.broadcast_to(ref[kind, pl.ds(pole, 1), :], (SEGS, HEAD))


def periodic_start(ends, par_ref, pole, backward):
    total = ends
    for power, kind in ((1, 3), (2, 4), (4, 5)):
        shift = SEGS - power if backward else power
        total = total + row_of(par_ref, kind, pole) * pltpu.roll(total, shift, 0)
    total = total * row_of(par_ref, 6, pole)
    return pltpu.roll(total, SEGS - 1 if backward else 1, 0)


def segment_ends(x_ref, par_ref, poles, steps, backward, unroll=4):
    lams = [row_of(par_ref, 0, pole) for pole in range(poles)]

    def body(index, states):
        for sub in range(unroll):
            step = index * unroll + sub
            if backward:
                step = steps - 1 - step
            x = x_ref[pl.ds(step, SEGS, stride=steps), :]
            states = tuple(lam * state + x for lam, state in zip(lams, states))
        return states

    zeros = tuple(jnp.zeros((SEGS, HEAD), jnp.float32) for _ in range(poles))
    ends = lax.fori_loop(0, steps // unroll, body, zeros)
    return [periodic_start(end, par_ref, pole, backward) for pole, end in enumerate(ends)]


def tree_sum(terms):
    terms = list(terms)
    while len(terms) > 1:
        paired = [a + b for a, b in zip(terms[::2], terms[1::2])]
        if len(terms) % 2:
            paired.append(terms[-1])
        terms = paired
    return terms[0]


def fast_kernel(
    members, local_heads,
    q_ref, k_ref, v_ref, gate_ref, cot_ref, decay_ref, residue_ref, skip_ref,
    dq_ref, dk_ref, dv_ref, dgate_ref, dres_ref,
    stage, inbox, outbox, landed, res_box, res_landed, res_wide,
    cot_v, gate_v, decay_v, residue_v, skip_v, par_ref, delta_ref, y_ref, att_ref, da_ref, dk_acc, dv_acc,
    in_send, in_recv, grad_send, grad_recv, mix_send, mix_recv, res_send, res_recv,
    load_sem, stage_sem, out_sem,
):
    me = lax.axis_index("ctx")
    rows = q_ref.shape[0]
    tokens = rows * members
    steps = tokens // SEGS
    poles = decay_v.shape[0]
    group = local_heads // members
    scale = 1.0 / math.sqrt(HEAD)

    owned = pl.ds(pl.multiple_of(me * (group * HEAD), HEAD), group * HEAD)
    loads = [
        pltpu.make_async_copy(src, dst, load_sem.at[index])
        for index, (src, dst) in enumerate((
            (cot_ref, cot_v), (gate_ref, gate_v), (decay_ref.at[:, owned], decay_v),
            (residue_ref.at[:, owned], residue_v), (skip_ref.at[:, owned], skip_v),
        ))
    ]
    for load in loads[:2]:
        load.start()

    def lanes(owner, head):
        return pl.ds(pl.multiple_of((owner * group + head) * HEAD, HEAD), HEAD)

    def stage_copy(head, owner, kind):
        return pltpu.make_async_copy(
            (q_ref, k_ref, v_ref)[kind].at[:, lanes(owner, head)],
            stage.at[head, owner, kind + 1], stage_sem.at[head, owner, kind],
        )

    def start_stage(head, carry):
        for owner in range(members):
            for kind in range(3):
                stage_copy(head, owner, kind).start()
        return carry

    start_stage(0, 0)
    barrier = pltpu.get_barrier_semaphore()
    for off in range(1, members):
        pl.semaphore_signal(
            barrier, inc=1, device_id={"ctx": lax.rem(me + off, members)}, device_id_type=MESH
        )
    lax.fori_loop(1, group, start_stage, 0)
    for load in loads[2:]:
        load.start()
    for load in loads[:2]:
        load.wait()
    pl.semaphore_wait(barrier, members - 1)

    def rows_of(owner):
        return pl.ds(pl.multiple_of(owner * rows, rows), rows)

    def dest(off):
        return lax.rem(me + off, members)

    def source(off):
        return lax.rem(me + members - off, members)

    def remote(src, dst, send, recv, target):
        return pltpu.make_async_remote_copy(
            src_ref=src, dst_ref=dst, send_sem=send, recv_sem=recv,
            device_id={"ctx": target}, device_id_type=MESH,
        )

    def in_copy(head, off):
        return remote(
            stage.at[head, dest(off)], inbox.at[head, :, rows_of(me), :],
            in_send.at[head, off - 1], in_recv.at[head, off - 1], dest(off),
        )

    def in_arrival(head, off):
        return remote(
            stage.at[head, dest(off)], inbox.at[head, :, rows_of(source(off)), :],
            in_send.at[head, off - 1], in_recv.at[head, off - 1], dest(off),
        )

    def grad_copy(head, off, owner):
        return remote(
            outbox.at[head, pl.ds(0, 3), rows_of(dest(off)), :],
            landed.at[head, owner, pl.ds(0, 3)],
            grad_send.at[head, off - 1], grad_recv.at[head, off - 1], dest(off),
        )

    def mix_copy(head, off, owner):
        return remote(
            outbox.at[head, pl.ds(3, 1), rows_of(dest(off)), :],
            landed.at[head, owner, pl.ds(3, 1)],
            mix_send.at[head, off - 1], mix_recv.at[head, off - 1], dest(off),
        )

    def res_copy(head, off, owner):
        return remote(
            res_box.at[head], res_landed.at[head, owner],
            res_send.at[head, off - 1], res_recv.at[head, off - 1], dest(off),
        )

    odd = lax.rem(me, 2)
    far_first = (2, 3 - 2 * odd, 1 + 2 * odd) if members == 4 else tuple(range(1, members))

    def send_inputs(head, carry):
        for owner in range(members):
            here = lanes(owner, head)
            stage[head, owner, 0] = (
                cot_v[:, here].astype(jnp.float32) * gate_v[:, here].astype(jnp.float32)
            ).astype(jnp.bfloat16)
            for kind in range(3):
                stage_copy(head, owner, kind).wait()
        for off in far_first:
            in_copy(head, off).start()
        return carry

    lax.fori_loop(0, group, send_inputs, 0)
    for load in loads[2:]:
        load.wait()

    def one_head(head, carry):
        mine = pl.ds(pl.multiple_of(head * HEAD, HEAD), HEAD)
        damping = decay_v[:, mine]
        weights = jnp.sqrt(decay_gap(2.0 * damping))
        par_ref[0] = 1.0 - decay_gap(damping)
        par_ref[1] = residue_v[:, mine] * weights
        par_ref[2] = weights
        par_ref[3] = jnp.exp(-damping * steps)
        par_ref[4] = jnp.exp(-damping * (2 * steps))
        par_ref[5] = jnp.exp(-damping * (4 * steps))
        par_ref[6] = 1.0 / (1.0 - jnp.exp(-damping * tokens))
        skip = jnp.broadcast_to(skip_v[:, mine], (SEGS, HEAD))
        inbox[head, :, rows_of(me), :] = stage[head, me]
        for off in range(1, members):
            in_arrival(head, off).wait_recv()
        delta_ref[...] = inbox[head, 0].astype(jnp.float32)

        entering = segment_ends(delta_ref, par_ref, poles, steps, True)
        lams = [row_of(par_ref, 0, pole) for pole in range(poles)]
        mixes = [row_of(par_ref, 1, pole) for pole in range(poles)]

        def backward_body(index, states):
            for sub in range(2):
                step = steps - 1 - (index * 2 + sub)
                x = delta_ref[pl.ds(step, SEGS, stride=steps), :]
                states = tuple(lam * state + x for lam, state in zip(lams, states))
                y_ref[pl.ds(step, SEGS, stride=steps), :] = skip * x + tree_sum(
                    mix * state for mix, state in zip(mixes, states)
                )
            return states

        lax.fori_loop(0, steps // 2, backward_body, tuple(entering))
        da_ref[...] = y_ref[...].astype(jnp.bfloat16)

        key_head = inbox[head, 2]
        value_head = inbox[head, 3]
        for block in range(members):
            span = pl.ds(block * rows, rows)
            query = inbox[head, 1, span, :]
            adjoint = da_ref[span, :]
            scores = lax.dot_general(
                query, key_head, (((1,), (1,)), ((), ())), preferred_element_type=jnp.float32
            ) * scale
            raised = jnp.exp(scores - jnp.max(scores, axis=1, keepdims=True))
            probability = raised * (1.0 / jnp.sum(raised, axis=1, keepdims=True))
            rounded = probability.astype(jnp.bfloat16)
            attended = jnp.dot(rounded, value_head, preferred_element_type=jnp.float32)
            att_ref[span, :] = attended.astype(jnp.bfloat16).astype(jnp.float32)
            weight_adjoint = lax.dot_general(
                adjoint, value_head, (((1,), (1,)), ((), ())), preferred_element_type=jnp.float32
            )
            inner = jnp.sum(probability * weight_adjoint, axis=1, keepdims=True)
            score_adjoint = (probability * (weight_adjoint - inner) * scale).astype(jnp.bfloat16)
            outbox[head, 0, span, :] = jnp.dot(
                score_adjoint, key_head, preferred_element_type=jnp.float32
            ).astype(jnp.bfloat16)
            key_part = lax.dot_general(
                score_adjoint, query, (((0,), (0,)), ((), ())), preferred_element_type=jnp.float32
            )
            value_part = lax.dot_general(
                rounded, adjoint, (((0,), (0,)), ((), ())), preferred_element_type=jnp.float32
            )
            if block == 0:
                dk_acc[...] = key_part
                dv_acc[...] = value_part
            else:
                dk_acc[...] += key_part
                dv_acc[...] += value_part
        outbox[head, 1] = dk_acc[...].astype(jnp.bfloat16)
        outbox[head, 2] = dv_acc[...].astype(jnp.bfloat16)
        for off in far_first:
            grad_copy(head, off, me).start()

        entering_forward = segment_ends(att_ref, par_ref, poles, steps, False)
        for first in range(0, poles, POLE_GROUP):
            chosen = range(first, first + POLE_GROUP)
            group_lams = [row_of(par_ref, 0, pole) for pole in chosen]
            group_mixes = [row_of(par_ref, 1, pole) for pole in chosen]

            def forward_body(index, item, first=first, lams=group_lams, mixes=group_mixes):
                states, sums = item
                for sub in range(2):
                    step = index * 2 + sub
                    here = pl.ds(step, SEGS, stride=steps)
                    x = att_ref[here, :]
                    delta = delta_ref[here, :]
                    states = tuple(lam * state + x for lam, state in zip(lams, states))
                    sums = tuple(total + delta * state for total, state in zip(sums, states))
                    base = skip * x if first == 0 else y_ref[here, :]
                    y_ref[here, :] = base + tree_sum(
                        mix * state for mix, state in zip(mixes, states)
                    )
                return states, sums

            zeros = tuple(jnp.zeros((SEGS, HEAD), jnp.float32) for _ in chosen)
            starts = tuple(entering_forward[pole] for pole in chosen)
            unused, sums = lax.fori_loop(0, steps // 2, forward_body, (starts, zeros))
            for pole, total in zip(chosen, sums):
                par_ref[7, pl.ds(pole, 1), :] = (
                    jnp.sum(total, axis=0, keepdims=True) * par_ref[2, pl.ds(pole, 1), :]
                )
        res_box[head] = par_ref[7].astype(jnp.bfloat16)
        outbox[head, 3] = y_ref[...].astype(jnp.bfloat16)
        for off in far_first:
            mix_copy(head, off, me).start()
            res_copy(head, off, me).start()
        landed[head, me] = outbox[head, :, rows_of(me), :]
        res_landed[head, me] = res_box[head]
        return carry

    lax.fori_loop(0, group, one_head, 0)

    def out_copy(head, owner, kind):
        src = res_wide.at[head, owner] if kind == 4 else landed.at[head, owner, kind]
        target = (dq_ref, dk_ref, dv_ref, dgate_ref, dres_ref)[kind]
        return pltpu.make_async_copy(
            src, target.at[:, lanes(owner, head)], out_sem.at[head, owner, kind]
        )

    def finish(head, carry):
        for off in range(1, members):
            grad_copy(head, off, source(off)).wait_recv()
            mix_copy(head, off, source(off)).wait_recv()
            res_copy(head, off, source(off)).wait_recv()
        for owner in range(members):
            landed[head, owner, 3] = (
                cot_v[:, lanes(owner, head)].astype(jnp.float32)
                * landed[head, owner, 3].astype(jnp.float32)
            ).astype(jnp.bfloat16)
            res_wide[head, owner] = res_landed[head, owner].astype(jnp.float32)
            for kind in range(5):
                out_copy(head, owner, kind).start()
        return carry

    lax.fori_loop(0, group, finish, 0)
    def sent(head, carry):
        for off in range(1, members):
            in_copy(head, off).wait_send()
            grad_copy(head, off, me).wait_send()
            mix_copy(head, off, me).wait_send()
            res_copy(head, off, me).wait_send()
        for owner in range(members):
            for kind in range(5):
                out_copy(head, owner, kind).wait()
        return carry

    lax.fori_loop(0, group, sent, 0)


def write_kernel(*refs):
    sources, targets, sem = refs[:5], refs[5:10], refs[10]
    copies = []
    for src, dst in zip(sources, targets):
        width = src.shape[1] // 2
        for half in range(2):
            part = pl.ds(half * width, width)
            copies.append(
                pltpu.make_async_copy(src.at[:, part], dst.at[:, part], sem.at[len(copies)])
            )
    for copy in copies:
        copy.start()
    for copy in copies:
        copy.wait()


def fast_local(queries, key_rows, value_rows, gate_values, cotangent, decay_rates, residues, skip_gain):
    members = lax.axis_size("ctx")
    rows, channels = queries.shape
    local_heads = channels // HEAD
    group = local_heads // members
    tokens = rows * members
    poles = decay_rates.shape[0]
    wide = jax.ShapeDtypeStruct((rows, channels), jnp.bfloat16)
    sems = pltpu.SemaphoreType.DMA((group, members - 1))
    hbm = pl.BlockSpec(memory_space=pltpu.HBM)
    shapes = (wide, wide, wide, wide, jax.ShapeDtypeStruct((poles, channels), jnp.float32))
    results = pl.pallas_call(
        functools.partial(fast_kernel, members, local_heads),
        out_shape=shapes,
        in_specs=[hbm] * 8,
        out_specs=(hbm,) * 5,
        scratch_shapes=[
            pltpu.VMEM((group, members, 4, rows, HEAD), jnp.bfloat16),
            pltpu.VMEM((group, 4, tokens, HEAD), jnp.bfloat16),
            pltpu.VMEM((group, 4, tokens, HEAD), jnp.bfloat16),
            pltpu.VMEM((group, members, 4, rows, HEAD), jnp.bfloat16),
            pltpu.VMEM((group, poles, HEAD), jnp.bfloat16),
            pltpu.VMEM((group, members, poles, HEAD), jnp.bfloat16),
            pltpu.VMEM((group, members, poles, HEAD), jnp.float32),
            pltpu.VMEM((rows, channels), jnp.bfloat16),
            pltpu.VMEM((rows, channels), jnp.bfloat16),
            pltpu.VMEM((poles, group * HEAD), jnp.float32),
            pltpu.VMEM((poles, group * HEAD), jnp.float32),
            pltpu.VMEM((1, group * HEAD), jnp.float32),
            pltpu.VMEM((8, poles, HEAD), jnp.float32),
            pltpu.VMEM((tokens, HEAD), jnp.float32),
            pltpu.VMEM((tokens, HEAD), jnp.float32),
            pltpu.VMEM((tokens, HEAD), jnp.float32),
            pltpu.VMEM((tokens, HEAD), jnp.bfloat16),
            pltpu.VMEM((tokens, HEAD), jnp.float32),
            pltpu.VMEM((tokens, HEAD), jnp.float32),
        ] + [sems] * 8 + [
            pltpu.SemaphoreType.DMA((5,)), pltpu.SemaphoreType.DMA((group, members, 3)),
            pltpu.SemaphoreType.DMA((group, members, 5)),
        ],
        compiler_params=pltpu.CompilerParams(
            collective_id=0, has_side_effects=True, vmem_limit_bytes=60 * 1024 * 1024
        ),
    )(queries, key_rows, value_rows, gate_values, cotangent, decay_rates, residues,
      skip_gain.reshape(1, channels))
    return pl.pallas_call(
        write_kernel,
        out_shape=shapes,
        in_specs=[hbm] * 5,
        out_specs=(hbm,) * 5,
        scratch_shapes=[pltpu.SemaphoreType.DMA((10,))],
        compiler_params=pltpu.CompilerParams(vmem_limit_bytes=60 * 1024 * 1024),
    )(*results)


def passed_along(array, axis, by):
    length = lax.axis_size(axis)
    return lax.ppermute(array, axis, [(i, (i + by) % length) for i in range(length)])


def window_mask(row_count):
    row_ids = jnp.arange(row_count)[:, None, None]
    lag_ids = jnp.arange(WIN + 1)[None, :, None]
    column_ids = jnp.arange(row_count)[None, None, :]
    return ((lag_ids > 0) | (column_ids <= row_ids)) & ((lag_ids < WIN) | (column_ids > row_ids))


def local(queries, key_rows, value_rows, gate_values, cotangent, decay_rates, residues, skip_gain):
    members = lax.axis_size("ctx")
    tok_rows, channels = queries.shape
    local_heads = channels // HEAD
    scale_factor = 1.0 / math.sqrt(HEAD)
    weights = jnp.sqrt(-jnp.expm1(-2.0 * decay_rates))
    mixing = residues * weights
    loop_gap = -jnp.expm1(-decay_rates * (tok_rows * members))
    device_decay = jnp.exp(-decay_rates * tok_rows)
    piece_rows = min(128, tok_rows)
    pieces = tok_rows // piece_rows
    offsets = jnp.arange(piece_rows, dtype=jnp.float32)[:, None, None]
    piece_index = jnp.arange(pieces, dtype=jnp.float32)[:, None, None]
    start_weights = jnp.exp(-decay_rates[None] * offsets)
    growth = jnp.exp(decay_rates[None] * offsets)
    delta_rows = cotangent.astype(jnp.float32) * gate_values.astype(jnp.float32)
    blocks_delta = delta_rows.reshape(pieces, piece_rows, channels)
    piece_starts = jnp.einsum(
        "qpc,mqc->mpc", start_weights, blocks_delta, precision=lax.Precision.HIGHEST
    )
    head_state = jnp.sum(
        jnp.exp(-decay_rates[None] * (piece_index * piece_rows)) * piece_starts, axis=0
    )

    def backward_turn(turn_index, moving):
        return passed_along(device_decay * moving + head_state, "ctx", -1)

    incoming = lax.fori_loop(0, members, backward_turn, jnp.zeros_like(head_state)) / loop_gap

    def backward_step(carried, segment):
        local_part = growth * lax.cumsum(start_weights * segment[:, None, :], axis=0, reverse=True)
        states = local_part + jnp.exp(-decay_rates[None] * (piece_rows - offsets)) * carried[None]
        mixture = jnp.sum(mixing[None] * states, axis=1) + skip_gain[None] * segment
        return (states[0], mixture)

    unused_state, adjoint_rows = lax.scan(backward_step, incoming, blocks_delta, reverse=True)
    attended_adjoint = adjoint_rows.reshape(tok_rows, channels).astype(jnp.bfloat16)
    key_value = jnp.stack([key_rows, value_rows])
    window = [key_value]
    moving = key_value
    for lag_index in range(WIN):
        moving = passed_along(moving, "ctx", 1)
        window.append(moving)
    stacked = jnp.stack(window)
    key_window = stacked[:, 0]
    value_window = stacked[:, 1]
    allowed = window_mask(tok_rows)
    attended_parts = []
    query_adjoints = []
    key_partials = []
    value_partials = []
    for head_index in range(local_heads):
        first = head_index * HEAD
        query_head = queries[:, first : first + HEAD]
        key_head = key_window[:, :, first : first + HEAD]
        value_head = value_window[:, :, first : first + HEAD]
        adjoint_head = attended_adjoint[:, first : first + HEAD]
        scores = (
            jnp.einsum("re,kse->rks", query_head, key_head, preferred_element_type=jnp.float32)
            * scale_factor
        )
        masked = jnp.where(allowed, scores, -jnp.inf)
        row_top = jnp.max(masked, axis=(1, 2), keepdims=True)
        raised = jnp.exp(masked - row_top)
        probability = raised / jnp.sum(raised, axis=(1, 2), keepdims=True)
        rounded_prob = probability.astype(jnp.bfloat16)
        attended_parts.append(
            jnp.einsum(
                "rks,kse->re", rounded_prob, value_head, preferred_element_type=jnp.float32
            ).astype(jnp.bfloat16)
        )
        weight_adjoint = jnp.einsum(
            "re,kse->rks", adjoint_head, value_head, preferred_element_type=jnp.float32
        )
        inner_sum = jnp.sum(probability * weight_adjoint, axis=(1, 2), keepdims=True)
        score_adjoint = (probability * (weight_adjoint - inner_sum) * scale_factor).astype(
            jnp.bfloat16
        )
        query_adjoints.append(
            jnp.einsum(
                "rks,kse->re", score_adjoint, key_head, preferred_element_type=jnp.float32
            ).astype(jnp.bfloat16)
        )
        key_partials.append(
            jnp.einsum(
                "rks,re->kse", score_adjoint, query_head, preferred_element_type=jnp.float32
            ).astype(jnp.bfloat16)
        )
        value_partials.append(
            jnp.einsum(
                "rks,re->kse", rounded_prob, adjoint_head, preferred_element_type=jnp.float32
            ).astype(jnp.bfloat16)
        )
    attended = jnp.concatenate(attended_parts, axis=1)
    queries_adjoint = jnp.concatenate(query_adjoints, axis=1)
    partials = jnp.stack(
        [jnp.concatenate(key_partials, axis=2), jnp.concatenate(value_partials, axis=2)], axis=1
    )
    collected = partials[0].astype(jnp.float32)
    for lag_index in range(1, WIN + 1):
        collected = collected + passed_along(partials[lag_index], "ctx", -lag_index).astype(
            jnp.float32
        )
    keys_adjoint = collected[0].astype(jnp.bfloat16)
    values_adjoint = collected[1].astype(jnp.bfloat16)
    signal = attended.astype(jnp.float32)
    blocks_signal = signal.reshape(pieces, piece_rows, channels)
    end_weights = jnp.exp(-decay_rates[None] * (piece_rows - 1.0 - offsets))
    piece_ends = jnp.einsum(
        "qpc,mqc->mpc", end_weights, blocks_signal, precision=lax.Precision.HIGHEST
    )
    tail_state = jnp.sum(
        jnp.exp(-decay_rates[None] * ((pieces - 1.0 - piece_index) * piece_rows)) * piece_ends,
        axis=0,
    )

    def forward_turn(turn_index, moving):
        return passed_along(device_decay * moving + tail_state, "ctx", 1)

    arriving = lax.fori_loop(0, members, forward_turn, jnp.zeros_like(tail_state)) / loop_gap
    entering = jnp.exp(-decay_rates[None] * (offsets + 1.0))

    def forward_step(carried, step_item):
        segment, matched = step_item
        local_part = start_weights * jnp.cumsum(growth * segment[:, None, :], axis=0)
        states = local_part + entering * carried[None]
        mixture = jnp.sum(mixing[None] * states, axis=1) + skip_gain[None] * segment
        product = jnp.sum(weights[None] * matched[:, None, :] * states, axis=0)
        return (states[-1], (mixture, product))

    closing, (mixed_rows, products) = lax.scan(
        forward_step, arriving, (blocks_signal, blocks_delta)
    )
    gate_adjoint = (cotangent.astype(jnp.float32) * mixed_rows.reshape(tok_rows, channels)).astype(
        jnp.bfloat16
    )
    residues_adjoint = lax.psum(jnp.sum(products, axis=0), "ctx")
    return (queries_adjoint, keys_adjoint, values_adjoint, gate_adjoint, residues_adjoint)


def solution(mesh):
    in_specs = (
        P(("dp", "ctx"), "head"),
        P(("dp", "ctx"), "head"),
        P(("dp", "ctx"), "head"),
        P(("dp", "ctx"), "head"),
        P(("dp", "ctx"), "head"),
        P(None, "head"),
        P(None, "head"),
        P("head"),
    )
    out_specs = (
        P(("dp", "ctx"), "head"),
        P(("dp", "ctx"), "head"),
        P(("dp", "ctx"), "head"),
        P(("dp", "ctx"), "head"),
        P("dp", "head"),
    )
    members = mesh.shape["ctx"]

    def chosen(*arrays):
        rows, channels = arrays[0].shape
        whole = members == WIN and rows % 128 == 0 and (channels // HEAD) % members == 0
        return (fast_local if whole and arrays[5].shape[0] % POLE_GROUP == 0 else local)(*arrays)

    return jax.shard_map(chosen, mesh=mesh, in_specs=in_specs, out_specs=out_specs, check_vma=False)
```

```python
import functools
import math

import jax
import jax.numpy as jnp
from jax import lax
from jax.experimental import pallas as pl
from jax.experimental.pallas import tpu as pltpu
from jax.sharding import PartitionSpec as P

HEAD = 128
WIN = 4
SEGS = 8
POLE_GROUP = 8
AHEAD = 2
MESH = pl.DeviceIdType.MESH


def decay_gap(x):
    inner = 1.0 - x * (1.0 / 7.0)
    for order in (6.0, 5.0, 4.0, 3.0, 2.0):
        inner = 1.0 - x * (1.0 / order) * inner
    return x * inner


def row_of(ref, kind, pole):
    return jnp.broadcast_to(ref[kind, pl.ds(pole, 1), :], (SEGS, HEAD))


def periodic_start(ends, par_ref, pole, backward):
    total = ends
    for power, kind in ((1, 3), (2, 4), (4, 5)):
        shift = SEGS - power if backward else power
        total = total + row_of(par_ref, kind, pole) * pltpu.roll(total, shift, 0)
    total = total * row_of(par_ref, 6, pole)
    return pltpu.roll(total, SEGS - 1 if backward else 1, 0)


def segment_ends(x_ref, par_ref, poles, steps, backward, unroll=4):
    lams = [row_of(par_ref, 0, pole) for pole in range(poles)]

    def body(index, states):
        for sub in range(unroll):
            step = index * unroll + sub
            if backward:
                step = steps - 1 - step
            x = x_ref[pl.ds(step, SEGS, stride=steps), :]
            states = tuple(lam * state + x for lam, state in zip(lams, states))
        return states

    zeros = tuple(jnp.zeros((SEGS, HEAD), jnp.float32) for _ in range(poles))
    ends = lax.fori_loop(0, steps // unroll, body, zeros)
    return [periodic_start(end, par_ref, pole, backward) for pole, end in enumerate(ends)]


def tree_sum(terms):
    terms = list(terms)
    while len(terms) > 1:
        paired = [a + b for a, b in zip(terms[::2], terms[1::2])]
        if len(terms) % 2:
            paired.append(terms[-1])
        terms = paired
    return terms[0]


def fast_kernel(
    members, local_heads,
    q_ref, k_ref, v_ref, gate_ref, cot_ref, decay_ref, residue_ref, skip_ref,
    dq_ref, dk_ref, dv_ref, dgate_ref, dres_ref,
    stage, inbox, outbox, landed, res_box, res_landed, res_wide,
    cot_v, gate_v, decay_v, residue_v, skip_v, par_ref, delta_ref, y_ref, att_ref, da_ref, dk_acc, dv_acc,
    in_send, in_recv, grad_send, grad_recv, mix_send, mix_recv, res_send, res_recv,
    load_sem, stage_sem, out_sem,
):
    me = lax.axis_index("ctx")
    rows = q_ref.shape[0]
    tokens = rows * members
    steps = tokens // SEGS
    poles = decay_v.shape[0]
    group = local_heads // members
    scale = 1.0 / math.sqrt(HEAD)

    owned = pl.ds(pl.multiple_of(me * (group * HEAD), HEAD), group * HEAD)
    loads = [
        pltpu.make_async_copy(src, dst, load_sem.at[index])
        for index, (src, dst) in enumerate((
            (cot_ref, cot_v), (gate_ref, gate_v), (decay_ref.at[:, owned], decay_v),
            (residue_ref.at[:, owned], residue_v), (skip_ref.at[:, owned], skip_v),
        ))
    ]
    for load in loads[:2]:
        load.start()

    def lanes(owner, head):
        return pl.ds(pl.multiple_of((owner * group + head) * HEAD, HEAD), HEAD)

    def stage_copy(head, owner, kind):
        return pltpu.make_async_copy(
            (q_ref, k_ref, v_ref)[kind].at[:, lanes(owner, head)],
            stage.at[head, owner, kind + 1], stage_sem.at[head, owner, kind],
        )

    def start_stage(head, carry):
        for owner in range(members):
            for kind in range(3):
                stage_copy(head, owner, kind).start()
        return carry

    start_stage(0, 0)
    barrier = pltpu.get_barrier_semaphore()
    for off in range(1, members):
        pl.semaphore_signal(
            barrier, inc=1, device_id={"ctx": lax.rem(me + off, members)}, device_id_type=MESH
        )
    lax.fori_loop(1, group, start_stage, 0)
    for load in loads[2:]:
        load.start()
    for load in loads[:2]:
        load.wait()
    pl.semaphore_wait(barrier, members - 1)

    def rows_of(owner):
        return pl.ds(pl.multiple_of(owner * rows, rows), rows)

    def dest(off):
        return lax.rem(me + off, members)

    def source(off):
        return lax.rem(me + members - off, members)

    def remote(src, dst, send, recv, target):
        return pltpu.make_async_remote_copy(
            src_ref=src, dst_ref=dst, send_sem=send, recv_sem=recv,
            device_id={"ctx": target}, device_id_type=MESH,
        )

    def in_copy(head, off):
        return remote(
            stage.at[head, dest(off)], inbox.at[head, :, rows_of(me), :],
            in_send.at[head, off - 1], in_recv.at[head, off - 1], dest(off),
        )

    def in_arrival(head, off):
        return remote(
            stage.at[head, dest(off)], inbox.at[head, :, rows_of(source(off)), :],
            in_send.at[head, off - 1], in_recv.at[head, off - 1], dest(off),
        )

    def grad_copy(head, off, owner):
        return remote(
            outbox.at[head, pl.ds(0, 3), rows_of(dest(off)), :],
            landed.at[head, owner, pl.ds(0, 3)],
            grad_send.at[head, off - 1], grad_recv.at[head, off - 1], dest(off),
        )

    def mix_copy(head, off, owner):
        return remote(
            outbox.at[head, pl.ds(3, 1), rows_of(dest(off)), :],
            landed.at[head, owner, pl.ds(3, 1)],
            mix_send.at[head, off - 1], mix_recv.at[head, off - 1], dest(off),
        )

    def res_copy(head, off, owner):
        return remote(
            res_box.at[head], res_landed.at[head, owner],
            res_send.at[head, off - 1], res_recv.at[head, off - 1], dest(off),
        )

    odd = lax.rem(me, 2)
    far_first = (2, 3 - 2 * odd, 1 + 2 * odd) if members == 4 else tuple(range(1, members))

    def send_inputs(head, carry):
        for owner in range(members):
            here = lanes(owner, head)
            stage[head, owner, 0] = (
                cot_v[:, here].astype(jnp.float32) * gate_v[:, here].astype(jnp.float32)
            ).astype(jnp.bfloat16)
            for kind in range(3):
                stage_copy(head, owner, kind).wait()
        for off in far_first:
            in_copy(head, off).start()
        return carry

    lax.fori_loop(0, min(AHEAD, group), send_inputs, 0)
    for load in loads[2:]:
        load.wait()

    def one_head(head, carry):
        mine = pl.ds(pl.multiple_of(head * HEAD, HEAD), HEAD)
        damping = decay_v[:, mine]
        weights = jnp.sqrt(decay_gap(2.0 * damping))
        par_ref[0] = 1.0 - decay_gap(damping)
        par_ref[1] = residue_v[:, mine] * weights
        par_ref[2] = weights
        par_ref[3] = jnp.exp(-damping * steps)
        par_ref[4] = jnp.exp(-damping * (2 * steps))
        par_ref[5] = jnp.exp(-damping * (4 * steps))
        par_ref[6] = 1.0 / (1.0 - jnp.exp(-damping * tokens))
        skip = jnp.broadcast_to(skip_v[:, mine], (SEGS, HEAD))
        inbox[head, :, rows_of(me), :] = stage[head, me]
        for off in range(1, members):
            in_arrival(head, off).wait_recv()

        @pl.when(head + AHEAD < group)
        def _():
            send_inputs(head + AHEAD, 0)

        delta_ref[...] = inbox[head, 0].astype(jnp.float32)

        entering = segment_ends(delta_ref, par_ref, poles, steps, True)
        lams = [row_of(par_ref, 0, pole) for pole in range(poles)]
        mixes = [row_of(par_ref, 1, pole) for pole in range(poles)]

        def backward_body(index, states):
            for sub in range(2):
                step = steps - 1 - (index * 2 + sub)
                x = delta_ref[pl.ds(step, SEGS, stride=steps), :]
                states = tuple(lam * state + x for lam, state in zip(lams, states))
                y_ref[pl.ds(step, SEGS, stride=steps), :] = skip * x + tree_sum(
                    mix * state for mix, state in zip(mixes, states)
                )
            return states

        lax.fori_loop(0, steps // 2, backward_body, tuple(entering))
        da_ref[...] = y_ref[...].astype(jnp.bfloat16)

        key_head = inbox[head, 2]
        value_head = inbox[head, 3]
        for block in range(members):
            span = pl.ds(block * rows, rows)
            query = inbox[head, 1, span, :]
            adjoint = da_ref[span, :]
            scores = lax.dot_general(
                query, key_head, (((1,), (1,)), ((), ())), preferred_element_type=jnp.float32
            ) * scale
            raised = jnp.exp(scores - jnp.max(scores, axis=1, keepdims=True))
            probability = raised * (1.0 / jnp.sum(raised, axis=1, keepdims=True))
            rounded = probability.astype(jnp.bfloat16)
            attended = jnp.dot(rounded, value_head, preferred_element_type=jnp.float32)
            att_ref[span, :] = attended.astype(jnp.bfloat16).astype(jnp.float32)
            weight_adjoint = lax.dot_general(
                adjoint, value_head, (((1,), (1,)), ((), ())), preferred_element_type=jnp.float32
            )
            inner = jnp.sum(probability * weight_adjoint, axis=1, keepdims=True)
            score_adjoint = (probability * (weight_adjoint - inner) * scale).astype(jnp.bfloat16)
            outbox[head, 0, span, :] = jnp.dot(
                score_adjoint, key_head, preferred_element_type=jnp.float32
            ).astype(jnp.bfloat16)
            key_part = lax.dot_general(
                score_adjoint, query, (((0,), (0,)), ((), ())), preferred_element_type=jnp.float32
            )
            value_part = lax.dot_general(
                rounded, adjoint, (((0,), (0,)), ((), ())), preferred_element_type=jnp.float32
            )
            if block == 0:
                dk_acc[...] = key_part
                dv_acc[...] = value_part
            else:
                dk_acc[...] += key_part
                dv_acc[...] += value_part
        outbox[head, 1] = dk_acc[...].astype(jnp.bfloat16)
        outbox[head, 2] = dv_acc[...].astype(jnp.bfloat16)
        for off in far_first:
            grad_copy(head, off, me).start()

        entering_forward = segment_ends(att_ref, par_ref, poles, steps, False)
        for first in range(0, poles, POLE_GROUP):
            chosen = range(first, first + POLE_GROUP)
            group_lams = [row_of(par_ref, 0, pole) for pole in chosen]
            group_mixes = [row_of(par_ref, 1, pole) for pole in chosen]

            def forward_body(index, item, first=first, lams=group_lams, mixes=group_mixes):
                states, sums = item
                for sub in range(2):
                    step = index * 2 + sub
                    here = pl.ds(step, SEGS, stride=steps)
                    x = att_ref[here, :]
                    delta = delta_ref[here, :]
                    states = tuple(lam * state + x for lam, state in zip(lams, states))
                    sums = tuple(total + delta * state for total, state in zip(sums, states))
                    base = skip * x if first == 0 else y_ref[here, :]
                    y_ref[here, :] = base + tree_sum(
                        mix * state for mix, state in zip(mixes, states)
                    )
                return states, sums

            zeros = tuple(jnp.zeros((SEGS, HEAD), jnp.float32) for _ in chosen)
            starts = tuple(entering_forward[pole] for pole in chosen)
            unused, sums = lax.fori_loop(0, steps // 2, forward_body, (starts, zeros))
            for pole, total in zip(chosen, sums):
                par_ref[7, pl.ds(pole, 1), :] = (
                    jnp.sum(total, axis=0, keepdims=True) * par_ref[2, pl.ds(pole, 1), :]
                )
        res_box[head] = par_ref[7].astype(jnp.bfloat16)
        outbox[head, 3] = y_ref[...].astype(jnp.bfloat16)
        for off in far_first:
            mix_copy(head, off, me).start()
            res_copy(head, off, me).start()
        landed[head, me] = outbox[head, :, rows_of(me), :]
        res_landed[head, me] = res_box[head]
        return carry

    lax.fori_loop(0, group, one_head, 0)

    def out_copy(head, owner, kind):
        src = res_wide.at[head, owner] if kind == 4 else landed.at[head, owner, kind]
        target = (dq_ref, dk_ref, dv_ref, dgate_ref, dres_ref)[kind]
        return pltpu.make_async_copy(
            src, target.at[:, lanes(owner, head)], out_sem.at[head, owner, kind]
        )

    def finish(head, carry):
        for off in range(1, members):
            grad_copy(head, off, source(off)).wait_recv()
            mix_copy(head, off, source(off)).wait_recv()
            res_copy(head, off, source(off)).wait_recv()
        for owner in range(members):
            landed[head, owner, 3] = (
                cot_v[:, lanes(owner, head)].astype(jnp.float32)
                * landed[head, owner, 3].astype(jnp.float32)
            ).astype(jnp.bfloat16)
            res_wide[head, owner] = res_landed[head, owner].astype(jnp.float32)
            for kind in range(5):
                out_copy(head, owner, kind).start()
        return carry

    lax.fori_loop(0, group, finish, 0)
    def sent(head, carry):
        for off in range(1, members):
            in_copy(head, off).wait_send()
            grad_copy(head, off, me).wait_send()
            mix_copy(head, off, me).wait_send()
            res_copy(head, off, me).wait_send()
        for owner in range(members):
            for kind in range(5):
                out_copy(head, owner, kind).wait()
        return carry

    lax.fori_loop(0, group, sent, 0)


def write_kernel(*refs):
    sources, targets, held, in_sem, out_sem = refs[:5], refs[5:10], refs[10:15], refs[15], refs[16]
    loads, stores = [], []
    for src, dst, middle in zip(sources, targets, held):
        width = src.shape[1] // 2
        for half in range(2):
            part = pl.ds(half * width, width)
            index = len(loads)
            loads.append(
                pltpu.make_async_copy(src.at[:, part], middle.at[:, part], in_sem.at[index])
            )
            stores.append(
                pltpu.make_async_copy(middle.at[:, part], dst.at[:, part], out_sem.at[index])
            )
    for load in loads:
        load.start()
    for load, store in zip(loads, stores):
        load.wait()
        store.start()
    for store in stores:
        store.wait()


def fast_local(queries, key_rows, value_rows, gate_values, cotangent, decay_rates, residues, skip_gain):
    members = lax.axis_size("ctx")
    rows, channels = queries.shape
    local_heads = channels // HEAD
    group = local_heads // members
    tokens = rows * members
    poles = decay_rates.shape[0]
    wide = jax.ShapeDtypeStruct((rows, channels), jnp.bfloat16)
    sems = pltpu.SemaphoreType.DMA((group, members - 1))
    hbm = pl.BlockSpec(memory_space=pltpu.HBM)
    shapes = (wide, wide, wide, wide, jax.ShapeDtypeStruct((poles, channels), jnp.float32))
    results = pl.pallas_call(
        functools.partial(fast_kernel, members, local_heads),
        out_shape=shapes,
        in_specs=[hbm] * 8,
        out_specs=(hbm,) * 5,
        scratch_shapes=[
            pltpu.VMEM((group, members, 4, rows, HEAD), jnp.bfloat16),
            pltpu.VMEM((group, 4, tokens, HEAD), jnp.bfloat16),
            pltpu.VMEM((group, 4, tokens, HEAD), jnp.bfloat16),
            pltpu.VMEM((group, members, 4, rows, HEAD), jnp.bfloat16),
            pltpu.VMEM((group, poles, HEAD), jnp.bfloat16),
            pltpu.VMEM((group, members, poles, HEAD), jnp.bfloat16),
            pltpu.VMEM((group, members, poles, HEAD), jnp.float32),
            pltpu.VMEM((rows, channels), jnp.bfloat16),
            pltpu.VMEM((rows, channels), jnp.bfloat16),
            pltpu.VMEM((poles, group * HEAD), jnp.float32),
            pltpu.VMEM((poles, group * HEAD), jnp.float32),
            pltpu.VMEM((1, group * HEAD), jnp.float32),
            pltpu.VMEM((8, poles, HEAD), jnp.float32),
            pltpu.VMEM((tokens, HEAD), jnp.float32),
            pltpu.VMEM((tokens, HEAD), jnp.float32),
            pltpu.VMEM((tokens, HEAD), jnp.float32),
            pltpu.VMEM((tokens, HEAD), jnp.bfloat16),
            pltpu.VMEM((tokens, HEAD), jnp.float32),
            pltpu.VMEM((tokens, HEAD), jnp.float32),
        ] + [sems] * 8 + [
            pltpu.SemaphoreType.DMA((5,)), pltpu.SemaphoreType.DMA((group, members, 3)),
            pltpu.SemaphoreType.DMA((group, members, 5)),
        ],
        compiler_params=pltpu.CompilerParams(
            collective_id=0, has_side_effects=True, vmem_limit_bytes=60 * 1024 * 1024
        ),
    )(queries, key_rows, value_rows, gate_values, cotangent, decay_rates, residues,
      skip_gain.reshape(1, channels))
    return pl.pallas_call(
        write_kernel,
        out_shape=shapes,
        in_specs=[hbm] * 5,
        out_specs=(hbm,) * 5,
        scratch_shapes=[pltpu.VMEM(shape.shape, shape.dtype) for shape in shapes]
        + [pltpu.SemaphoreType.DMA((10,))] * 2,
        compiler_params=pltpu.CompilerParams(vmem_limit_bytes=60 * 1024 * 1024),
    )(*results)


def passed_along(array, axis, by):
    length = lax.axis_size(axis)
    return lax.ppermute(array, axis, [(i, (i + by) % length) for i in range(length)])


def window_mask(row_count):
    row_ids = jnp.arange(row_count)[:, None, None]
    lag_ids = jnp.arange(WIN + 1)[None, :, None]
    column_ids = jnp.arange(row_count)[None, None, :]
    return ((lag_ids > 0) | (column_ids <= row_ids)) & ((lag_ids < WIN) | (column_ids > row_ids))


def local(queries, key_rows, value_rows, gate_values, cotangent, decay_rates, residues, skip_gain):
    members = lax.axis_size("ctx")
    tok_rows, channels = queries.shape
    local_heads = channels // HEAD
    scale_factor = 1.0 / math.sqrt(HEAD)
    weights = jnp.sqrt(-jnp.expm1(-2.0 * decay_rates))
    mixing = residues * weights
    loop_gap = -jnp.expm1(-decay_rates * (tok_rows * members))
    device_decay = jnp.exp(-decay_rates * tok_rows)
    piece_rows = min(128, tok_rows)
    pieces = tok_rows // piece_rows
    offsets = jnp.arange(piece_rows, dtype=jnp.float32)[:, None, None]
    piece_index = jnp.arange(pieces, dtype=jnp.float32)[:, None, None]
    start_weights = jnp.exp(-decay_rates[None] * offsets)
    growth = jnp.exp(decay_rates[None] * offsets)
    delta_rows = cotangent.astype(jnp.float32) * gate_values.astype(jnp.float32)
    blocks_delta = delta_rows.reshape(pieces, piece_rows, channels)
    piece_starts = jnp.einsum(
        "qpc,mqc->mpc", start_weights, blocks_delta, precision=lax.Precision.HIGHEST
    )
    head_state = jnp.sum(
        jnp.exp(-decay_rates[None] * (piece_index * piece_rows)) * piece_starts, axis=0
    )

    def backward_turn(turn_index, moving):
        return passed_along(device_decay * moving + head_state, "ctx", -1)

    incoming = lax.fori_loop(0, members, backward_turn, jnp.zeros_like(head_state)) / loop_gap

    def backward_step(carried, segment):
        local_part = growth * lax.cumsum(start_weights * segment[:, None, :], axis=0, reverse=True)
        states = local_part + jnp.exp(-decay_rates[None] * (piece_rows - offsets)) * carried[None]
        mixture = jnp.sum(mixing[None] * states, axis=1) + skip_gain[None] * segment
        return (states[0], mixture)

    unused_state, adjoint_rows = lax.scan(backward_step, incoming, blocks_delta, reverse=True)
    attended_adjoint = adjoint_rows.reshape(tok_rows, channels).astype(jnp.bfloat16)
    key_value = jnp.stack([key_rows, value_rows])
    window = [key_value]
    moving = key_value
    for lag_index in range(WIN):
        moving = passed_along(moving, "ctx", 1)
        window.append(moving)
    stacked = jnp.stack(window)
    key_window = stacked[:, 0]
    value_window = stacked[:, 1]
    allowed = window_mask(tok_rows)
    attended_parts = []
    query_adjoints = []
    key_partials = []
    value_partials = []
    for head_index in range(local_heads):
        first = head_index * HEAD
        query_head = queries[:, first : first + HEAD]
        key_head = key_window[:, :, first : first + HEAD]
        value_head = value_window[:, :, first : first + HEAD]
        adjoint_head = attended_adjoint[:, first : first + HEAD]
        scores = (
            jnp.einsum("re,kse->rks", query_head, key_head, preferred_element_type=jnp.float32)
            * scale_factor
        )
        masked = jnp.where(allowed, scores, -jnp.inf)
        row_top = jnp.max(masked, axis=(1, 2), keepdims=True)
        raised = jnp.exp(masked - row_top)
        probability = raised / jnp.sum(raised, axis=(1, 2), keepdims=True)
        rounded_prob = probability.astype(jnp.bfloat16)
        attended_parts.append(
            jnp.einsum(
                "rks,kse->re", rounded_prob, value_head, preferred_element_type=jnp.float32
            ).astype(jnp.bfloat16)
        )
        weight_adjoint = jnp.einsum(
            "re,kse->rks", adjoint_head, value_head, preferred_element_type=jnp.float32
        )
        inner_sum = jnp.sum(probability * weight_adjoint, axis=(1, 2), keepdims=True)
        score_adjoint = (probability * (weight_adjoint - inner_sum) * scale_factor).astype(
            jnp.bfloat16
        )
        query_adjoints.append(
            jnp.einsum(
                "rks,kse->re", score_adjoint, key_head, preferred_element_type=jnp.float32
            ).astype(jnp.bfloat16)
        )
        key_partials.append(
            jnp.einsum(
                "rks,re->kse", score_adjoint, query_head, preferred_element_type=jnp.float32
            ).astype(jnp.bfloat16)
        )
        value_partials.append(
            jnp.einsum(
                "rks,re->kse", rounded_prob, adjoint_head, preferred_element_type=jnp.float32
            ).astype(jnp.bfloat16)
        )
    attended = jnp.concatenate(attended_parts, axis=1)
    queries_adjoint = jnp.concatenate(query_adjoints, axis=1)
    partials = jnp.stack(
        [jnp.concatenate(key_partials, axis=2), jnp.concatenate(value_partials, axis=2)], axis=1
    )
    collected = partials[0].astype(jnp.float32)
    for lag_index in range(1, WIN + 1):
        collected = collected + passed_along(partials[lag_index], "ctx", -lag_index).astype(
            jnp.float32
        )
    keys_adjoint = collected[0].astype(jnp.bfloat16)
    values_adjoint = collected[1].astype(jnp.bfloat16)
    signal = attended.astype(jnp.float32)
    blocks_signal = signal.reshape(pieces, piece_rows, channels)
    end_weights = jnp.exp(-decay_rates[None] * (piece_rows - 1.0 - offsets))
    piece_ends = jnp.einsum(
        "qpc,mqc->mpc", end_weights, blocks_signal, precision=lax.Precision.HIGHEST
    )
    tail_state = jnp.sum(
        jnp.exp(-decay_rates[None] * ((pieces - 1.0 - piece_index) * piece_rows)) * piece_ends,
        axis=0,
    )

    def forward_turn(turn_index, moving):
        return passed_along(device_decay * moving + tail_state, "ctx", 1)

    arriving = lax.fori_loop(0, members, forward_turn, jnp.zeros_like(tail_state)) / loop_gap
    entering = jnp.exp(-decay_rates[None] * (offsets + 1.0))

    def forward_step(carried, step_item):
        segment, matched = step_item
        local_part = start_weights * jnp.cumsum(growth * segment[:, None, :], axis=0)
        states = local_part + entering * carried[None]
        mixture = jnp.sum(mixing[None] * states, axis=1) + skip_gain[None] * segment
        product = jnp.sum(weights[None] * matched[:, None, :] * states, axis=0)
        return (states[-1], (mixture, product))

    closing, (mixed_rows, products) = lax.scan(
        forward_step, arriving, (blocks_signal, blocks_delta)
    )
    gate_adjoint = (cotangent.astype(jnp.float32) * mixed_rows.reshape(tok_rows, channels)).astype(
        jnp.bfloat16
    )
    residues_adjoint = lax.psum(jnp.sum(products, axis=0), "ctx")
    return (queries_adjoint, keys_adjoint, values_adjoint, gate_adjoint, residues_adjoint)


def solution(mesh):
    in_specs = (
        P(("dp", "ctx"), "head"),
        P(("dp", "ctx"), "head"),
        P(("dp", "ctx"), "head"),
        P(("dp", "ctx"), "head"),
        P(("dp", "ctx"), "head"),
        P(None, "head"),
        P(None, "head"),
        P("head"),
    )
    out_specs = (
        P(("dp", "ctx"), "head"),
        P(("dp", "ctx"), "head"),
        P(("dp", "ctx"), "head"),
        P(("dp", "ctx"), "head"),
        P("dp", "head"),
    )
    members = mesh.shape["ctx"]

    def chosen(*arrays):
        rows, channels = arrays[0].shape
        whole = members == WIN and rows % 128 == 0 and (channels // HEAD) % members == 0
        return (fast_local if whole and arrays[5].shape[0] % POLE_GROUP == 0 else local)(*arrays)

    return jax.shard_map(chosen, mesh=mesh, in_specs=in_specs, out_specs=out_specs, check_vma=False)
```

```python
import functools
import math

import jax
import jax.numpy as jnp
from jax import lax
from jax.experimental import pallas as pl
from jax.experimental.pallas import tpu as pltpu
from jax.sharding import PartitionSpec as P

HEAD = 128
WIN = 4
SEGS = 8
POLE_GROUP = 8
AHEAD = 2
MESH = pl.DeviceIdType.MESH


def decay_gap(x):
    inner = 1.0 - x * (1.0 / 7.0)
    for order in (6.0, 5.0, 4.0, 3.0, 2.0):
        inner = 1.0 - x * (1.0 / order) * inner
    return x * inner


def row_of(ref, kind, pole):
    return jnp.broadcast_to(ref[kind, pl.ds(pole, 1), :], (SEGS, HEAD))


def periodic_start(ends, par_ref, pole, backward):
    total = ends
    for power, kind in ((1, 3), (2, 4), (4, 5)):
        shift = SEGS - power if backward else power
        total = total + row_of(par_ref, kind, pole) * pltpu.roll(total, shift, 0)
    total = total * row_of(par_ref, 6, pole)
    return pltpu.roll(total, SEGS - 1 if backward else 1, 0)


def segment_ends(x_ref, par_ref, poles, steps, backward, unroll=4):
    lams = [row_of(par_ref, 0, pole) for pole in range(poles)]

    def body(index, states):
        for sub in range(unroll):
            step = index * unroll + sub
            if backward:
                step = steps - 1 - step
            x = x_ref[pl.ds(step, SEGS, stride=steps + 1), :]
            states = tuple(lam * state + x for lam, state in zip(lams, states))
        return states

    zeros = tuple(jnp.zeros((SEGS, HEAD), jnp.float32) for _ in range(poles))
    ends = lax.fori_loop(0, steps // unroll, body, zeros)
    return [periodic_start(end, par_ref, pole, backward) for pole, end in enumerate(ends)]


def tree_sum(terms):
    terms = list(terms)
    while len(terms) > 1:
        paired = [a + b for a, b in zip(terms[::2], terms[1::2])]
        if len(terms) % 2:
            paired.append(terms[-1])
        terms = paired
    return terms[0]


def fast_kernel(
    members, local_heads,
    q_ref, k_ref, v_ref, gate_ref, cot_ref, decay_ref, residue_ref, skip_ref,
    dq_ref, dk_ref, dv_ref, dgate_ref, dres_ref,
    stage, inbox, outbox, landed, res_box, res_landed, res_wide,
    cot_v, gate_v, decay_v, residue_v, skip_v, par_ref, delta_ref, y_ref, att_ref, da_ref, dk_acc, dv_acc,
    in_send, in_recv, grad_send, grad_recv, mix_send, mix_recv, res_send, res_recv,
    load_sem, stage_sem, out_sem,
):
    me = lax.axis_index("ctx")
    rows = q_ref.shape[0]
    tokens = rows * members
    steps = tokens // SEGS
    poles = decay_v.shape[0]
    group = local_heads // members
    scale = 1.0 / math.sqrt(HEAD)

    barrier = pltpu.get_barrier_semaphore()
    for off in range(1, members):
        pl.semaphore_signal(
            barrier, inc=1, device_id={"ctx": lax.rem(me + off, members)}, device_id_type=MESH
        )
    owned = pl.ds(pl.multiple_of(me * (group * HEAD), HEAD), group * HEAD)
    loads = [
        pltpu.make_async_copy(src, dst, load_sem.at[index])
        for index, (src, dst) in enumerate((
            (cot_ref, cot_v), (gate_ref, gate_v), (decay_ref.at[:, owned], decay_v),
            (residue_ref.at[:, owned], residue_v), (skip_ref.at[:, owned], skip_v),
        ))
    ]
    for load in loads[:2]:
        load.start()

    def lanes(owner, head):
        return pl.ds(pl.multiple_of((owner * group + head) * HEAD, HEAD), HEAD)

    def stage_copy(head, owner, kind):
        return pltpu.make_async_copy(
            (q_ref, k_ref, v_ref)[kind].at[:, lanes(owner, head)],
            stage.at[head, owner, kind + 1], stage_sem.at[head, owner, kind],
        )

    def start_stage(head, carry):
        for owner in range(members):
            for kind in range(3):
                stage_copy(head, owner, kind).start()
        return carry

    start_stage(0, 0)
    lax.fori_loop(1, group, start_stage, 0)
    for load in loads[2:]:
        load.start()
    for load in loads[:2]:
        load.wait()
    pl.semaphore_wait(barrier, members - 1)

    def rows_of(owner):
        return pl.ds(pl.multiple_of(owner * rows, rows), rows)

    def dest(off):
        return lax.rem(me + off, members)

    def source(off):
        return lax.rem(me + members - off, members)

    def remote(src, dst, send, recv, target):
        return pltpu.make_async_remote_copy(
            src_ref=src, dst_ref=dst, send_sem=send, recv_sem=recv,
            device_id={"ctx": target}, device_id_type=MESH,
        )

    def in_copy(head, off):
        return remote(
            stage.at[head, dest(off)], inbox.at[head, :, rows_of(me), :],
            in_send.at[head, off - 1], in_recv.at[head, off - 1], dest(off),
        )

    def in_arrival(head, off):
        return remote(
            stage.at[head, dest(off)], inbox.at[head, :, rows_of(source(off)), :],
            in_send.at[head, off - 1], in_recv.at[head, off - 1], dest(off),
        )

    def grad_copy(head, off, owner):
        return remote(
            outbox.at[head, pl.ds(0, 3), rows_of(dest(off)), :],
            landed.at[head, owner, pl.ds(0, 3)],
            grad_send.at[head, off - 1], grad_recv.at[head, off - 1], dest(off),
        )

    def mix_copy(head, off, owner):
        return remote(
            outbox.at[head, pl.ds(3, 1), rows_of(dest(off)), :],
            landed.at[head, owner, pl.ds(3, 1)],
            mix_send.at[head, off - 1], mix_recv.at[head, off - 1], dest(off),
        )

    def res_copy(head, off, owner):
        return remote(
            res_box.at[head], res_landed.at[head, owner],
            res_send.at[head, off - 1], res_recv.at[head, off - 1], dest(off),
        )

    odd = lax.rem(me, 2)
    far_first = (2, 3 - 2 * odd, 1 + 2 * odd) if members == 4 else tuple(range(1, members))

    def send_inputs(head, carry):
        for owner in range(members):
            here = lanes(owner, head)
            stage[head, owner, 0] = (
                cot_v[:, here].astype(jnp.float32) * gate_v[:, here].astype(jnp.float32)
            ).astype(jnp.bfloat16)
            for kind in range(3):
                stage_copy(head, owner, kind).wait()
        for off in far_first:
            in_copy(head, off).start()
        return carry

    lax.fori_loop(0, min(AHEAD, group), send_inputs, 0)
    for load in loads[2:]:
        load.wait()

    def one_head(head, carry):
        mine = pl.ds(pl.multiple_of(head * HEAD, HEAD), HEAD)
        damping = decay_v[:, mine]
        weights = jnp.sqrt(decay_gap(2.0 * damping))
        par_ref[0] = 1.0 - decay_gap(damping)
        par_ref[1] = residue_v[:, mine] * weights
        par_ref[2] = weights
        par_ref[3] = jnp.exp(-damping * steps)
        par_ref[4] = jnp.exp(-damping * (2 * steps))
        par_ref[5] = jnp.exp(-damping * (4 * steps))
        par_ref[6] = 1.0 / (1.0 - jnp.exp(-damping * tokens))
        skip = jnp.broadcast_to(skip_v[:, mine], (SEGS, HEAD))
        inbox[head, :, rows_of(me), :] = stage[head, me]
        for off in range(1, members):
            in_arrival(head, off).wait_recv()

        @pl.when(head + AHEAD < group)
        def _():
            send_inputs(head + AHEAD, 0)

        for seg in range(SEGS):
            delta_ref[pl.ds(seg * (steps + 1), steps), :] = inbox[
                head, 0, pl.ds(seg * steps, steps), :
            ].astype(jnp.float32)

        entering = segment_ends(delta_ref, par_ref, poles, steps, True)
        lams = [row_of(par_ref, 0, pole) for pole in range(poles)]
        mixes = [row_of(par_ref, 1, pole) for pole in range(poles)]

        def backward_body(index, states):
            for sub in range(2):
                step = steps - 1 - (index * 2 + sub)
                x = delta_ref[pl.ds(step, SEGS, stride=steps + 1), :]
                states = tuple(lam * state + x for lam, state in zip(lams, states))
                y_ref[pl.ds(step, SEGS, stride=steps + 1), :] = skip * x + tree_sum(
                    mix * state for mix, state in zip(mixes, states)
                )
            return states

        lax.fori_loop(0, steps // 2, backward_body, tuple(entering))
        for seg in range(SEGS):
            da_ref[pl.ds(seg * steps, steps), :] = y_ref[
                pl.ds(seg * (steps + 1), steps), :
            ].astype(jnp.bfloat16)

        key_head = inbox[head, 2]
        value_head = inbox[head, 3]
        for block in range(members):
            span = pl.ds(block * rows, rows)
            query = inbox[head, 1, span, :]
            adjoint = da_ref[span, :]
            scores = lax.dot_general(
                query, key_head, (((1,), (1,)), ((), ())), preferred_element_type=jnp.float32
            ) * scale
            raised = jnp.exp(scores - jnp.max(scores, axis=1, keepdims=True))
            probability = raised * (1.0 / jnp.sum(raised, axis=1, keepdims=True))
            rounded = probability.astype(jnp.bfloat16)
            attended = jnp.dot(rounded, value_head, preferred_element_type=jnp.float32)
            attended = attended.astype(jnp.bfloat16).astype(jnp.float32)
            for part in range(rows // steps):
                seg = block * (rows // steps) + part
                att_ref[pl.ds(seg * (steps + 1), steps), :] = attended[
                    part * steps : (part + 1) * steps
                ]
            weight_adjoint = lax.dot_general(
                adjoint, value_head, (((1,), (1,)), ((), ())), preferred_element_type=jnp.float32
            )
            inner = jnp.sum(probability * weight_adjoint, axis=1, keepdims=True)
            score_adjoint = (probability * (weight_adjoint - inner) * scale).astype(jnp.bfloat16)
            outbox[head, 0, span, :] = jnp.dot(
                score_adjoint, key_head, preferred_element_type=jnp.float32
            ).astype(jnp.bfloat16)
            key_part = lax.dot_general(
                score_adjoint, query, (((0,), (0,)), ((), ())), preferred_element_type=jnp.float32
            )
            value_part = lax.dot_general(
                rounded, adjoint, (((0,), (0,)), ((), ())), preferred_element_type=jnp.float32
            )
            if block == 0:
                dk_acc[...] = key_part
                dv_acc[...] = value_part
            else:
                dk_acc[...] += key_part
                dv_acc[...] += value_part
        outbox[head, 1] = dk_acc[...].astype(jnp.bfloat16)
        outbox[head, 2] = dv_acc[...].astype(jnp.bfloat16)
        for off in far_first:
            grad_copy(head, off, me).start()

        entering_forward = segment_ends(att_ref, par_ref, poles, steps, False)
        for first in range(0, poles, POLE_GROUP):
            chosen = range(first, first + POLE_GROUP)
            group_lams = [row_of(par_ref, 0, pole) for pole in chosen]
            group_mixes = [row_of(par_ref, 1, pole) for pole in chosen]

            def forward_body(index, item, first=first, lams=group_lams, mixes=group_mixes):
                states, sums = item
                for sub in range(2):
                    step = index * 2 + sub
                    here = pl.ds(step, SEGS, stride=steps + 1)
                    x = att_ref[here, :]
                    delta = delta_ref[here, :]
                    states = tuple(lam * state + x for lam, state in zip(lams, states))
                    sums = tuple(total + delta * state for total, state in zip(sums, states))
                    base = skip * x if first == 0 else y_ref[here, :]
                    y_ref[here, :] = base + tree_sum(
                        mix * state for mix, state in zip(mixes, states)
                    )
                return states, sums

            zeros = tuple(jnp.zeros((SEGS, HEAD), jnp.float32) for _ in chosen)
            starts = tuple(entering_forward[pole] for pole in chosen)
            unused, sums = lax.fori_loop(0, steps // 2, forward_body, (starts, zeros))
            for pole, total in zip(chosen, sums):
                par_ref[7, pl.ds(pole, 1), :] = (
                    jnp.sum(total, axis=0, keepdims=True) * par_ref[2, pl.ds(pole, 1), :]
                )
        res_box[head] = par_ref[7].astype(jnp.bfloat16)
        for seg in range(SEGS):
            outbox[head, 3, pl.ds(seg * steps, steps), :] = y_ref[
                pl.ds(seg * (steps + 1), steps), :
            ].astype(jnp.bfloat16)
        for off in far_first:
            mix_copy(head, off, me).start()
            res_copy(head, off, me).start()
        landed[head, me] = outbox[head, :, rows_of(me), :]
        res_landed[head, me] = res_box[head]
        return carry

    lax.fori_loop(0, group, one_head, 0)

    def out_copy(head, owner, kind):
        src = res_wide.at[head, owner] if kind == 4 else landed.at[head, owner, kind]
        target = (dq_ref, dk_ref, dv_ref, dgate_ref, dres_ref)[kind]
        return pltpu.make_async_copy(
            src, target.at[:, lanes(owner, head)], out_sem.at[head, owner, kind]
        )

    def finish(head, carry):
        for off in range(1, members):
            grad_copy(head, off, source(off)).wait_recv()
        for owner in range(members):
            for kind in range(3):
                out_copy(head, owner, kind).start()
        for off in range(1, members):
            mix_copy(head, off, source(off)).wait_recv()
            res_copy(head, off, source(off)).wait_recv()
        for owner in range(members):
            landed[head, owner, 3] = (
                cot_v[:, lanes(owner, head)].astype(jnp.float32)
                * landed[head, owner, 3].astype(jnp.float32)
            ).astype(jnp.bfloat16)
            res_wide[head, owner] = res_landed[head, owner].astype(jnp.float32)
            for kind in range(3, 5):
                out_copy(head, owner, kind).start()
        return carry

    lax.fori_loop(0, group, finish, 0)
    def sent(head, carry):
        for off in range(1, members):
            in_copy(head, off).wait_send()
            grad_copy(head, off, me).wait_send()
            mix_copy(head, off, me).wait_send()
            res_copy(head, off, me).wait_send()
        for owner in range(members):
            for kind in range(5):
                out_copy(head, owner, kind).wait()
        return carry

    lax.fori_loop(0, group, sent, 0)


def write_kernel(*refs):
    sources, targets, held, in_sem, out_sem = refs[:5], refs[5:10], refs[10:15], refs[15], refs[16]
    loads, stores = [], []
    for src, dst, middle in zip(sources, targets, held):
        pieces = 4 if src.shape[0] % 64 == 0 else 1
        height = src.shape[0] // pieces
        for piece in range(pieces):
            part = pl.ds(piece * height, height)
            index = len(loads)
            loads.append(pltpu.make_async_copy(src.at[part], middle.at[part], in_sem.at[index]))
            stores.append(pltpu.make_async_copy(middle.at[part], dst.at[part], out_sem.at[index]))
    for load in loads:
        load.start()
    for load, store in zip(loads, stores):
        load.wait()
        store.start()
    for store in stores:
        store.wait()


def fast_local(queries, key_rows, value_rows, gate_values, cotangent, decay_rates, residues, skip_gain):
    members = lax.axis_size("ctx")
    rows, channels = queries.shape
    local_heads = channels // HEAD
    group = local_heads // members
    tokens = rows * members
    poles = decay_rates.shape[0]
    wide = jax.ShapeDtypeStruct((rows, channels), jnp.bfloat16)
    sems = pltpu.SemaphoreType.DMA((group, members - 1))
    hbm = pl.BlockSpec(memory_space=pltpu.HBM)
    shapes = (wide, wide, wide, wide, jax.ShapeDtypeStruct((poles, channels), jnp.float32))
    results = pl.pallas_call(
        functools.partial(fast_kernel, members, local_heads),
        out_shape=shapes,
        in_specs=[hbm] * 8,
        out_specs=(hbm,) * 5,
        scratch_shapes=[
            pltpu.VMEM((group, members, 4, rows, HEAD), jnp.bfloat16),
            pltpu.VMEM((group, 4, tokens, HEAD), jnp.bfloat16),
            pltpu.VMEM((group, 4, tokens, HEAD), jnp.bfloat16),
            pltpu.VMEM((group, members, 4, rows, HEAD), jnp.bfloat16),
            pltpu.VMEM((group, poles, HEAD), jnp.bfloat16),
            pltpu.VMEM((group, members, poles, HEAD), jnp.bfloat16),
            pltpu.VMEM((group, members, poles, HEAD), jnp.float32),
            pltpu.VMEM((rows, channels), jnp.bfloat16),
            pltpu.VMEM((rows, channels), jnp.bfloat16),
            pltpu.VMEM((poles, group * HEAD), jnp.float32),
            pltpu.VMEM((poles, group * HEAD), jnp.float32),
            pltpu.VMEM((1, group * HEAD), jnp.float32),
            pltpu.VMEM((8, poles, HEAD), jnp.float32),
            pltpu.VMEM((tokens + SEGS, HEAD), jnp.float32),
            pltpu.VMEM((tokens + SEGS, HEAD), jnp.float32),
            pltpu.VMEM((tokens + SEGS, HEAD), jnp.float32),
            pltpu.VMEM((tokens, HEAD), jnp.bfloat16),
            pltpu.VMEM((tokens, HEAD), jnp.float32),
            pltpu.VMEM((tokens, HEAD), jnp.float32),
        ] + [sems] * 8 + [
            pltpu.SemaphoreType.DMA((5,)), pltpu.SemaphoreType.DMA((group, members, 3)),
            pltpu.SemaphoreType.DMA((group, members, 5)),
        ],
        compiler_params=pltpu.CompilerParams(
            collective_id=0, has_side_effects=True, vmem_limit_bytes=60 * 1024 * 1024
        ),
    )(queries, key_rows, value_rows, gate_values, cotangent, decay_rates, residues,
      skip_gain.reshape(1, channels))
    return pl.pallas_call(
        write_kernel,
        out_shape=shapes,
        in_specs=[hbm] * 5,
        out_specs=(hbm,) * 5,
        scratch_shapes=[pltpu.VMEM(shape.shape, shape.dtype) for shape in shapes]
        + [pltpu.SemaphoreType.DMA((20,))] * 2,
        compiler_params=pltpu.CompilerParams(vmem_limit_bytes=60 * 1024 * 1024),
    )(*results)


def passed_along(array, axis, by):
    length = lax.axis_size(axis)
    return lax.ppermute(array, axis, [(i, (i + by) % length) for i in range(length)])


def window_mask(row_count):
    row_ids = jnp.arange(row_count)[:, None, None]
    lag_ids = jnp.arange(WIN + 1)[None, :, None]
    column_ids = jnp.arange(row_count)[None, None, :]
    return ((lag_ids > 0) | (column_ids <= row_ids)) & ((lag_ids < WIN) | (column_ids > row_ids))


def local(queries, key_rows, value_rows, gate_values, cotangent, decay_rates, residues, skip_gain):
    members = lax.axis_size("ctx")
    tok_rows, channels = queries.shape
    local_heads = channels // HEAD
    scale_factor = 1.0 / math.sqrt(HEAD)
    weights = jnp.sqrt(-jnp.expm1(-2.0 * decay_rates))
    mixing = residues * weights
    loop_gap = -jnp.expm1(-decay_rates * (tok_rows * members))
    device_decay = jnp.exp(-decay_rates * tok_rows)
    piece_rows = min(128, tok_rows)
    pieces = tok_rows // piece_rows
    offsets = jnp.arange(piece_rows, dtype=jnp.float32)[:, None, None]
    piece_index = jnp.arange(pieces, dtype=jnp.float32)[:, None, None]
    start_weights = jnp.exp(-decay_rates[None] * offsets)
    growth = jnp.exp(decay_rates[None] * offsets)
    delta_rows = cotangent.astype(jnp.float32) * gate_values.astype(jnp.float32)
    blocks_delta = delta_rows.reshape(pieces, piece_rows, channels)
    piece_starts = jnp.einsum(
        "qpc,mqc->mpc", start_weights, blocks_delta, precision=lax.Precision.HIGHEST
    )
    head_state = jnp.sum(
        jnp.exp(-decay_rates[None] * (piece_index * piece_rows)) * piece_starts, axis=0
    )

    def backward_turn(turn_index, moving):
        return passed_along(device_decay * moving + head_state, "ctx", -1)

    incoming = lax.fori_loop(0, members, backward_turn, jnp.zeros_like(head_state)) / loop_gap

    def backward_step(carried, segment):
        local_part = growth * lax.cumsum(start_weights * segment[:, None, :], axis=0, reverse=True)
        states = local_part + jnp.exp(-decay_rates[None] * (piece_rows - offsets)) * carried[None]
        mixture = jnp.sum(mixing[None] * states, axis=1) + skip_gain[None] * segment
        return (states[0], mixture)

    unused_state, adjoint_rows = lax.scan(backward_step, incoming, blocks_delta, reverse=True)
    attended_adjoint = adjoint_rows.reshape(tok_rows, channels).astype(jnp.bfloat16)
    key_value = jnp.stack([key_rows, value_rows])
    window = [key_value]
    moving = key_value
    for lag_index in range(WIN):
        moving = passed_along(moving, "ctx", 1)
        window.append(moving)
    stacked = jnp.stack(window)
    key_window = stacked[:, 0]
    value_window = stacked[:, 1]
    allowed = window_mask(tok_rows)
    attended_parts = []
    query_adjoints = []
    key_partials = []
    value_partials = []
    for head_index in range(local_heads):
        first = head_index * HEAD
        query_head = queries[:, first : first + HEAD]
        key_head = key_window[:, :, first : first + HEAD]
        value_head = value_window[:, :, first : first + HEAD]
        adjoint_head = attended_adjoint[:, first : first + HEAD]
        scores = (
            jnp.einsum("re,kse->rks", query_head, key_head, preferred_element_type=jnp.float32)
            * scale_factor
        )
        masked = jnp.where(allowed, scores, -jnp.inf)
        row_top = jnp.max(masked, axis=(1, 2), keepdims=True)
        raised = jnp.exp(masked - row_top)
        probability = raised / jnp.sum(raised, axis=(1, 2), keepdims=True)
        rounded_prob = probability.astype(jnp.bfloat16)
        attended_parts.append(
            jnp.einsum(
                "rks,kse->re", rounded_prob, value_head, preferred_element_type=jnp.float32
            ).astype(jnp.bfloat16)
        )
        weight_adjoint = jnp.einsum(
            "re,kse->rks", adjoint_head, value_head, preferred_element_type=jnp.float32
        )
        inner_sum = jnp.sum(probability * weight_adjoint, axis=(1, 2), keepdims=True)
        score_adjoint = (probability * (weight_adjoint - inner_sum) * scale_factor).astype(
            jnp.bfloat16
        )
        query_adjoints.append(
            jnp.einsum(
                "rks,kse->re", score_adjoint, key_head, preferred_element_type=jnp.float32
            ).astype(jnp.bfloat16)
        )
        key_partials.append(
            jnp.einsum(
                "rks,re->kse", score_adjoint, query_head, preferred_element_type=jnp.float32
            ).astype(jnp.bfloat16)
        )
        value_partials.append(
            jnp.einsum(
                "rks,re->kse", rounded_prob, adjoint_head, preferred_element_type=jnp.float32
            ).astype(jnp.bfloat16)
        )
    attended = jnp.concatenate(attended_parts, axis=1)
    queries_adjoint = jnp.concatenate(query_adjoints, axis=1)
    partials = jnp.stack(
        [jnp.concatenate(key_partials, axis=2), jnp.concatenate(value_partials, axis=2)], axis=1
    )
    collected = partials[0].astype(jnp.float32)
    for lag_index in range(1, WIN + 1):
        collected = collected + passed_along(partials[lag_index], "ctx", -lag_index).astype(
            jnp.float32
        )
    keys_adjoint = collected[0].astype(jnp.bfloat16)
    values_adjoint = collected[1].astype(jnp.bfloat16)
    signal = attended.astype(jnp.float32)
    blocks_signal = signal.reshape(pieces, piece_rows, channels)
    end_weights = jnp.exp(-decay_rates[None] * (piece_rows - 1.0 - offsets))
    piece_ends = jnp.einsum(
        "qpc,mqc->mpc", end_weights, blocks_signal, precision=lax.Precision.HIGHEST
    )
    tail_state = jnp.sum(
        jnp.exp(-decay_rates[None] * ((pieces - 1.0 - piece_index) * piece_rows)) * piece_ends,
        axis=0,
    )

    def forward_turn(turn_index, moving):
        return passed_along(device_decay * moving + tail_state, "ctx", 1)

    arriving = lax.fori_loop(0, members, forward_turn, jnp.zeros_like(tail_state)) / loop_gap
    entering = jnp.exp(-decay_rates[None] * (offsets + 1.0))

    def forward_step(carried, step_item):
        segment, matched = step_item
        local_part = start_weights * jnp.cumsum(growth * segment[:, None, :], axis=0)
        states = local_part + entering * carried[None]
        mixture = jnp.sum(mixing[None] * states, axis=1) + skip_gain[None] * segment
        product = jnp.sum(weights[None] * matched[:, None, :] * states, axis=0)
        return (states[-1], (mixture, product))

    closing, (mixed_rows, products) = lax.scan(
        forward_step, arriving, (blocks_signal, blocks_delta)
    )
    gate_adjoint = (cotangent.astype(jnp.float32) * mixed_rows.reshape(tok_rows, channels)).astype(
        jnp.bfloat16
    )
    residues_adjoint = lax.psum(jnp.sum(products, axis=0), "ctx")
    return (queries_adjoint, keys_adjoint, values_adjoint, gate_adjoint, residues_adjoint)


def solution(mesh):
    in_specs = (
        P(("dp", "ctx"), "head"),
        P(("dp", "ctx"), "head"),
        P(("dp", "ctx"), "head"),
        P(("dp", "ctx"), "head"),
        P(("dp", "ctx"), "head"),
        P(None, "head"),
        P(None, "head"),
        P("head"),
    )
    out_specs = (
        P(("dp", "ctx"), "head"),
        P(("dp", "ctx"), "head"),
        P(("dp", "ctx"), "head"),
        P(("dp", "ctx"), "head"),
        P("dp", "head"),
    )
    members = mesh.shape["ctx"]

    def chosen(*arrays):
        rows, channels = arrays[0].shape
        whole = members == WIN and rows % 128 == 0 and (channels // HEAD) % members == 0
        return (fast_local if whole and arrays[5].shape[0] % POLE_GROUP == 0 else local)(*arrays)

    return jax.shard_map(chosen, mesh=mesh, in_specs=in_specs, out_specs=out_specs, check_vma=False)
```

```python
import functools
import math

import jax
import jax.numpy as jnp
from jax import lax
from jax.experimental import pallas as pl
from jax.experimental.pallas import tpu as pltpu
from jax.sharding import PartitionSpec as P

HEAD = 128
WIN = 4
SEGS = 8
POLE_GROUP = 8
AHEAD = 2
MESH = pl.DeviceIdType.MESH


def decay_gap(x):
    inner = 1.0 - x * (1.0 / 7.0)
    for order in (6.0, 5.0, 4.0, 3.0, 2.0):
        inner = 1.0 - x * (1.0 / order) * inner
    return x * inner


def row_of(ref, kind, pole):
    return jnp.broadcast_to(ref[kind, pl.ds(pole, 1), :], (SEGS, HEAD))


def periodic_start(ends, par_ref, pole, backward):
    total = ends
    for power, kind in ((1, 3), (2, 4), (4, 5)):
        shift = SEGS - power if backward else power
        total = total + row_of(par_ref, kind, pole) * pltpu.roll(total, shift, 0)
    total = total * row_of(par_ref, 6, pole)
    return pltpu.roll(total, SEGS - 1 if backward else 1, 0)


def segment_ends(x_ref, par_ref, poles, steps, backward, unroll=4):
    lams = [row_of(par_ref, 0, pole) for pole in range(poles)]

    def body(index, states):
        for sub in range(unroll):
            step = index * unroll + sub
            if backward:
                step = steps - 1 - step
            x = x_ref[pl.ds(step, SEGS, stride=steps + 1), :]
            states = tuple(lam * state + x for lam, state in zip(lams, states))
        return states

    zeros = tuple(jnp.zeros((SEGS, HEAD), jnp.float32) for _ in range(poles))
    ends = lax.fori_loop(0, steps // unroll, body, zeros)
    return [periodic_start(end, par_ref, pole, backward) for pole, end in enumerate(ends)]


def tree_sum(terms):
    terms = list(terms)
    while len(terms) > 1:
        paired = [a + b for a, b in zip(terms[::2], terms[1::2])]
        if len(terms) % 2:
            paired.append(terms[-1])
        terms = paired
    return terms[0]


def fast_kernel(
    members, local_heads,
    q_ref, k_ref, v_ref, gate_ref, cot_ref, decay_ref, residue_ref, skip_ref,
    dq_ref, dk_ref, dv_ref, dgate_ref, dres_ref,
    stage, inbox, outbox, landed, res_box, res_landed, res_wide,
    cot_v, gate_v, decay_v, residue_v, skip_v, par_ref, delta_ref, y_ref, att_ref, da_ref, dk_acc, dv_acc,
    in_send, in_recv, grad_send, grad_recv, mix_send, mix_recv, res_send, res_recv,
    load_sem, stage_sem, out_sem,
):
    me = lax.axis_index("ctx")
    rows = q_ref.shape[0]
    tokens = rows * members
    steps = tokens // SEGS
    poles = decay_v.shape[0]
    group = local_heads // members
    scale = 1.0 / math.sqrt(HEAD)

    barrier = pltpu.get_barrier_semaphore()
    for off in range(1, members):
        pl.semaphore_signal(
            barrier, inc=1, device_id={"ctx": lax.rem(me + off, members)}, device_id_type=MESH
        )
    owned = pl.ds(pl.multiple_of(me * (group * HEAD), HEAD), group * HEAD)
    loads = [
        pltpu.make_async_copy(src, dst, load_sem.at[index])
        for index, (src, dst) in enumerate((
            (cot_ref, cot_v), (gate_ref, gate_v), (decay_ref.at[:, owned], decay_v),
            (residue_ref.at[:, owned], residue_v), (skip_ref.at[:, owned], skip_v),
        ))
    ]
    for load in loads[:2]:
        load.start()

    def lanes(owner, head):
        return pl.ds(pl.multiple_of((owner * group + head) * HEAD, HEAD), HEAD)

    def stage_copy(head, owner, kind):
        return pltpu.make_async_copy(
            (q_ref, k_ref, v_ref)[kind].at[:, lanes(owner, head)],
            stage.at[head, owner, kind + 1], stage_sem.at[head, owner, kind],
        )

    def start_stage(head, carry):
        for owner in range(members):
            for kind in range(3):
                stage_copy(head, owner, kind).start()
        return carry

    start_stage(0, 0)
    lax.fori_loop(1, group, start_stage, 0)
    for load in loads[2:]:
        load.start()
    for load in loads[:2]:
        load.wait()
    pl.semaphore_wait(barrier, members - 1)

    def rows_of(owner):
        return pl.ds(pl.multiple_of(owner * rows, rows), rows)

    def dest(off):
        return lax.rem(me + off, members)

    def source(off):
        return lax.rem(me + members - off, members)

    def remote(src, dst, send, recv, target):
        return pltpu.make_async_remote_copy(
            src_ref=src, dst_ref=dst, send_sem=send, recv_sem=recv,
            device_id={"ctx": target}, device_id_type=MESH,
        )

    def in_copy(head, off):
        return remote(
            stage.at[head, dest(off)], inbox.at[head, :, rows_of(me), :],
            in_send.at[head, off - 1], in_recv.at[head, off - 1], dest(off),
        )

    def in_arrival(head, off):
        return remote(
            stage.at[head, dest(off)], inbox.at[head, :, rows_of(source(off)), :],
            in_send.at[head, off - 1], in_recv.at[head, off - 1], dest(off),
        )

    def grad_copy(head, off, owner):
        return remote(
            outbox.at[head, pl.ds(0, 3), rows_of(dest(off)), :],
            landed.at[head, owner, pl.ds(0, 3)],
            grad_send.at[head, off - 1], grad_recv.at[head, off - 1], dest(off),
        )

    def mix_copy(head, off, owner):
        return remote(
            outbox.at[head, pl.ds(3, 1), rows_of(dest(off)), :],
            landed.at[head, owner, pl.ds(3, 1)],
            mix_send.at[head, off - 1], mix_recv.at[head, off - 1], dest(off),
        )

    def res_copy(head, off, owner):
        return remote(
            res_box.at[head], res_landed.at[head, owner],
            res_send.at[head, off - 1], res_recv.at[head, off - 1], dest(off),
        )

    order = tuple(range(1, members))
    if members == 4:
        odd = lax.rem(me, 2)
        turn = lax.rem(lax.axis_index("dp"), 2)
        near, far = 1 + 2 * odd, 3 - 2 * odd
        order = (2 + turn * (near - 2), far + turn * (2 - far), near + turn * (far - near))

    def send_inputs(head, carry):
        for owner in range(members):
            here = lanes(owner, head)
            stage[head, owner, 0] = (
                cot_v[:, here].astype(jnp.float32) * gate_v[:, here].astype(jnp.float32)
            ).astype(jnp.bfloat16)
            for kind in range(3):
                stage_copy(head, owner, kind).wait()
        for off in order:
            in_copy(head, off).start()
        return carry

    lax.fori_loop(0, min(AHEAD, group), send_inputs, 0)
    for load in loads[2:]:
        load.wait()

    def one_head(head, carry):
        mine = pl.ds(pl.multiple_of(head * HEAD, HEAD), HEAD)
        damping = decay_v[:, mine]
        weights = jnp.sqrt(decay_gap(2.0 * damping))
        par_ref[0] = 1.0 - decay_gap(damping)
        par_ref[1] = residue_v[:, mine] * weights
        par_ref[2] = weights
        par_ref[3] = jnp.exp(-damping * steps)
        par_ref[4] = jnp.exp(-damping * (2 * steps))
        par_ref[5] = jnp.exp(-damping * (4 * steps))
        par_ref[6] = 1.0 / (1.0 - jnp.exp(-damping * tokens))
        skip = jnp.broadcast_to(skip_v[:, mine], (SEGS, HEAD))
        inbox[head, :, rows_of(me), :] = stage[head, me]
        for off in range(1, members):
            in_arrival(head, off).wait_recv()

        @pl.when(head + AHEAD < group)
        def _():
            send_inputs(head + AHEAD, 0)

        for seg in range(SEGS):
            delta_ref[pl.ds(seg * (steps + 1), steps), :] = inbox[
                head, 0, pl.ds(seg * steps, steps), :
            ].astype(jnp.float32)

        entering = segment_ends(delta_ref, par_ref, poles, steps, True)
        lams = [row_of(par_ref, 0, pole) for pole in range(poles)]
        mixes = [row_of(par_ref, 1, pole) for pole in range(poles)]

        def backward_body(index, states):
            for sub in range(2):
                step = steps - 1 - (index * 2 + sub)
                x = delta_ref[pl.ds(step, SEGS, stride=steps + 1), :]
                states = tuple(lam * state + x for lam, state in zip(lams, states))
                y_ref[pl.ds(step, SEGS, stride=steps + 1), :] = skip * x + tree_sum(
                    mix * state for mix, state in zip(mixes, states)
                )
            return states

        lax.fori_loop(0, steps // 2, backward_body, tuple(entering))
        for seg in range(SEGS):
            da_ref[pl.ds(seg * steps, steps), :] = y_ref[
                pl.ds(seg * (steps + 1), steps), :
            ].astype(jnp.bfloat16)

        key_head = inbox[head, 2]
        value_head = inbox[head, 3]
        for block in range(members):
            span = pl.ds(block * rows, rows)
            query = inbox[head, 1, span, :]
            adjoint = da_ref[span, :]
            scores = lax.dot_general(
                query, key_head, (((1,), (1,)), ((), ())), preferred_element_type=jnp.float32
            ) * scale
            raised = jnp.exp(scores - jnp.max(scores, axis=1, keepdims=True))
            probability = raised * (1.0 / jnp.sum(raised, axis=1, keepdims=True))
            rounded = probability.astype(jnp.bfloat16)
            attended = jnp.dot(rounded, value_head, preferred_element_type=jnp.float32)
            attended = attended.astype(jnp.bfloat16).astype(jnp.float32)
            for part in range(rows // steps):
                seg = block * (rows // steps) + part
                att_ref[pl.ds(seg * (steps + 1), steps), :] = attended[
                    part * steps : (part + 1) * steps
                ]
            weight_adjoint = lax.dot_general(
                adjoint, value_head, (((1,), (1,)), ((), ())), preferred_element_type=jnp.float32
            )
            inner = jnp.sum(probability * weight_adjoint, axis=1, keepdims=True)
            score_adjoint = (probability * (weight_adjoint - inner) * scale).astype(jnp.bfloat16)
            outbox[head, 0, span, :] = jnp.dot(
                score_adjoint, key_head, preferred_element_type=jnp.float32
            ).astype(jnp.bfloat16)
            key_part = lax.dot_general(
                score_adjoint, query, (((0,), (0,)), ((), ())), preferred_element_type=jnp.float32
            )
            value_part = lax.dot_general(
                rounded, adjoint, (((0,), (0,)), ((), ())), preferred_element_type=jnp.float32
            )
            if block == 0:
                dk_acc[...] = key_part
                dv_acc[...] = value_part
            else:
                dk_acc[...] += key_part
                dv_acc[...] += value_part
        outbox[head, 1] = dk_acc[...].astype(jnp.bfloat16)
        outbox[head, 2] = dv_acc[...].astype(jnp.bfloat16)
        for off in order:
            grad_copy(head, off, me).start()

        entering_forward = segment_ends(att_ref, par_ref, poles, steps, False)
        for first in range(0, poles, POLE_GROUP):
            chosen = range(first, first + POLE_GROUP)
            group_lams = [row_of(par_ref, 0, pole) for pole in chosen]
            group_mixes = [row_of(par_ref, 1, pole) for pole in chosen]

            def forward_body(index, item, first=first, lams=group_lams, mixes=group_mixes):
                states, sums = item
                for sub in range(2):
                    step = index * 2 + sub
                    here = pl.ds(step, SEGS, stride=steps + 1)
                    x = att_ref[here, :]
                    delta = delta_ref[here, :]
                    states = tuple(lam * state + x for lam, state in zip(lams, states))
                    sums = tuple(total + delta * state for total, state in zip(sums, states))
                    base = skip * x if first == 0 else y_ref[here, :]
                    y_ref[here, :] = base + tree_sum(
                        mix * state for mix, state in zip(mixes, states)
                    )
                return states, sums

            zeros = tuple(jnp.zeros((SEGS, HEAD), jnp.float32) for _ in chosen)
            starts = tuple(entering_forward[pole] for pole in chosen)
            unused, sums = lax.fori_loop(0, steps // 2, forward_body, (starts, zeros))
            for pole, total in zip(chosen, sums):
                par_ref[7, pl.ds(pole, 1), :] = (
                    jnp.sum(total, axis=0, keepdims=True) * par_ref[2, pl.ds(pole, 1), :]
                )
        res_box[head] = par_ref[7].astype(jnp.bfloat16)
        for seg in range(SEGS):
            outbox[head, 3, pl.ds(seg * steps, steps), :] = y_ref[
                pl.ds(seg * (steps + 1), steps), :
            ].astype(jnp.bfloat16)
        for off in order:
            mix_copy(head, off, me).start()
            res_copy(head, off, me).start()
        landed[head, me] = outbox[head, :, rows_of(me), :]
        res_landed[head, me] = res_box[head]
        return carry

    lax.fori_loop(0, group, one_head, 0)

    def out_copy(head, owner, kind):
        src = res_wide.at[head, owner] if kind == 4 else landed.at[head, owner, kind]
        target = (dq_ref, dk_ref, dv_ref, dgate_ref, dres_ref)[kind]
        return pltpu.make_async_copy(
            src, target.at[:, lanes(owner, head)], out_sem.at[head, owner, kind]
        )

    def finish(head, carry):
        for off in range(1, members):
            grad_copy(head, off, source(off)).wait_recv()
        for owner in range(members):
            for kind in range(3):
                out_copy(head, owner, kind).start()
        for off in range(1, members):
            mix_copy(head, off, source(off)).wait_recv()
            res_copy(head, off, source(off)).wait_recv()
        for owner in range(members):
            landed[head, owner, 3] = (
                cot_v[:, lanes(owner, head)].astype(jnp.float32)
                * landed[head, owner, 3].astype(jnp.float32)
            ).astype(jnp.bfloat16)
            res_wide[head, owner] = res_landed[head, owner].astype(jnp.float32)
            for kind in range(3, 5):
                out_copy(head, owner, kind).start()
        return carry

    lax.fori_loop(0, group, finish, 0)
    def sent(head, carry):
        for off in range(1, members):
            in_copy(head, off).wait_send()
            grad_copy(head, off, me).wait_send()
            mix_copy(head, off, me).wait_send()
            res_copy(head, off, me).wait_send()
        for owner in range(members):
            for kind in range(5):
                out_copy(head, owner, kind).wait()
        return carry

    lax.fori_loop(0, group, sent, 0)


def write_kernel(*refs):
    sources, targets, held, in_sem, out_sem = refs[:5], refs[5:10], refs[10:15], refs[15], refs[16]
    loads, stores = [], []
    for src, dst, middle in zip(sources, targets, held):
        pieces = 1
        height = src.shape[0] // pieces
        for piece in range(pieces):
            part = pl.ds(piece * height, height)
            index = len(loads)
            loads.append(pltpu.make_async_copy(src.at[part], middle.at[part], in_sem.at[index]))
            stores.append(pltpu.make_async_copy(middle.at[part], dst.at[part], out_sem.at[index]))
    for load in loads:
        load.start()
    for load, store in zip(loads, stores):
        load.wait()
        store.start()
    for store in stores:
        store.wait()


def fast_local(queries, key_rows, value_rows, gate_values, cotangent, decay_rates, residues, skip_gain):
    members = lax.axis_size("ctx")
    rows, channels = queries.shape
    local_heads = channels // HEAD
    group = local_heads // members
    tokens = rows * members
    poles = decay_rates.shape[0]
    wide = jax.ShapeDtypeStruct((rows, channels), jnp.bfloat16)
    sems = pltpu.SemaphoreType.DMA((group, members - 1))
    hbm = pl.BlockSpec(memory_space=pltpu.HBM)
    shapes = (wide, wide, wide, wide, jax.ShapeDtypeStruct((poles, channels), jnp.float32))
    results = pl.pallas_call(
        functools.partial(fast_kernel, members, local_heads),
        out_shape=shapes,
        in_specs=[hbm] * 8,
        out_specs=(hbm,) * 5,
        scratch_shapes=[
            pltpu.VMEM((group, members, 4, rows, HEAD), jnp.bfloat16),
            pltpu.VMEM((group, 4, tokens, HEAD), jnp.bfloat16),
            pltpu.VMEM((group, 4, tokens, HEAD), jnp.bfloat16),
            pltpu.VMEM((group, members, 4, rows, HEAD), jnp.bfloat16),
            pltpu.VMEM((group, poles, HEAD), jnp.bfloat16),
            pltpu.VMEM((group, members, poles, HEAD), jnp.bfloat16),
            pltpu.VMEM((group, members, poles, HEAD), jnp.float32),
            pltpu.VMEM((rows, channels), jnp.bfloat16),
            pltpu.VMEM((rows, channels), jnp.bfloat16),
            pltpu.VMEM((poles, group * HEAD), jnp.float32),
            pltpu.VMEM((poles, group * HEAD), jnp.float32),
            pltpu.VMEM((1, group * HEAD), jnp.float32),
            pltpu.VMEM((8, poles, HEAD), jnp.float32),
            pltpu.VMEM((tokens + SEGS, HEAD), jnp.float32),
            pltpu.VMEM((tokens + SEGS, HEAD), jnp.float32),
            pltpu.VMEM((tokens + SEGS, HEAD), jnp.float32),
            pltpu.VMEM((tokens, HEAD), jnp.bfloat16),
            pltpu.VMEM((tokens, HEAD), jnp.float32),
            pltpu.VMEM((tokens, HEAD), jnp.float32),
        ] + [sems] * 8 + [
            pltpu.SemaphoreType.DMA((5,)), pltpu.SemaphoreType.DMA((group, members, 3)),
            pltpu.SemaphoreType.DMA((group, members, 5)),
        ],
        compiler_params=pltpu.CompilerParams(
            collective_id=0, has_side_effects=True, vmem_limit_bytes=60 * 1024 * 1024
        ),
    )(queries, key_rows, value_rows, gate_values, cotangent, decay_rates, residues,
      skip_gain.reshape(1, channels))
    return pl.pallas_call(
        write_kernel,
        out_shape=shapes,
        in_specs=[hbm] * 5,
        out_specs=(hbm,) * 5,
        scratch_shapes=[pltpu.VMEM(shape.shape, shape.dtype) for shape in shapes]
        + [pltpu.SemaphoreType.DMA((20,))] * 2,
        compiler_params=pltpu.CompilerParams(vmem_limit_bytes=60 * 1024 * 1024),
    )(*results)


def passed_along(array, axis, by):
    length = lax.axis_size(axis)
    return lax.ppermute(array, axis, [(i, (i + by) % length) for i in range(length)])


def window_mask(row_count):
    row_ids = jnp.arange(row_count)[:, None, None]
    lag_ids = jnp.arange(WIN + 1)[None, :, None]
    column_ids = jnp.arange(row_count)[None, None, :]
    return ((lag_ids > 0) | (column_ids <= row_ids)) & ((lag_ids < WIN) | (column_ids > row_ids))


def local(queries, key_rows, value_rows, gate_values, cotangent, decay_rates, residues, skip_gain):
    members = lax.axis_size("ctx")
    tok_rows, channels = queries.shape
    local_heads = channels // HEAD
    scale_factor = 1.0 / math.sqrt(HEAD)
    weights = jnp.sqrt(-jnp.expm1(-2.0 * decay_rates))
    mixing = residues * weights
    loop_gap = -jnp.expm1(-decay_rates * (tok_rows * members))
    device_decay = jnp.exp(-decay_rates * tok_rows)
    piece_rows = min(128, tok_rows)
    pieces = tok_rows // piece_rows
    offsets = jnp.arange(piece_rows, dtype=jnp.float32)[:, None, None]
    piece_index = jnp.arange(pieces, dtype=jnp.float32)[:, None, None]
    start_weights = jnp.exp(-decay_rates[None] * offsets)
    growth = jnp.exp(decay_rates[None] * offsets)
    delta_rows = cotangent.astype(jnp.float32) * gate_values.astype(jnp.float32)
    blocks_delta = delta_rows.reshape(pieces, piece_rows, channels)
    piece_starts = jnp.einsum(
        "qpc,mqc->mpc", start_weights, blocks_delta, precision=lax.Precision.HIGHEST
    )
    head_state = jnp.sum(
        jnp.exp(-decay_rates[None] * (piece_index * piece_rows)) * piece_starts, axis=0
    )

    def backward_turn(turn_index, moving):
        return passed_along(device_decay * moving + head_state, "ctx", -1)

    incoming = lax.fori_loop(0, members, backward_turn, jnp.zeros_like(head_state)) / loop_gap

    def backward_step(carried, segment):
        local_part = growth * lax.cumsum(start_weights * segment[:, None, :], axis=0, reverse=True)
        states = local_part + jnp.exp(-decay_rates[None] * (piece_rows - offsets)) * carried[None]
        mixture = jnp.sum(mixing[None] * states, axis=1) + skip_gain[None] * segment
        return (states[0], mixture)

    unused_state, adjoint_rows = lax.scan(backward_step, incoming, blocks_delta, reverse=True)
    attended_adjoint = adjoint_rows.reshape(tok_rows, channels).astype(jnp.bfloat16)
    key_value = jnp.stack([key_rows, value_rows])
    window = [key_value]
    moving = key_value
    for lag_index in range(WIN):
        moving = passed_along(moving, "ctx", 1)
        window.append(moving)
    stacked = jnp.stack(window)
    key_window = stacked[:, 0]
    value_window = stacked[:, 1]
    allowed = window_mask(tok_rows)
    attended_parts = []
    query_adjoints = []
    key_partials = []
    value_partials = []
    for head_index in range(local_heads):
        first = head_index * HEAD
        query_head = queries[:, first : first + HEAD]
        key_head = key_window[:, :, first : first + HEAD]
        value_head = value_window[:, :, first : first + HEAD]
        adjoint_head = attended_adjoint[:, first : first + HEAD]
        scores = (
            jnp.einsum("re,kse->rks", query_head, key_head, preferred_element_type=jnp.float32)
            * scale_factor
        )
        masked = jnp.where(allowed, scores, -jnp.inf)
        row_top = jnp.max(masked, axis=(1, 2), keepdims=True)
        raised = jnp.exp(masked - row_top)
        probability = raised / jnp.sum(raised, axis=(1, 2), keepdims=True)
        rounded_prob = probability.astype(jnp.bfloat16)
        attended_parts.append(
            jnp.einsum(
                "rks,kse->re", rounded_prob, value_head, preferred_element_type=jnp.float32
            ).astype(jnp.bfloat16)
        )
        weight_adjoint = jnp.einsum(
            "re,kse->rks", adjoint_head, value_head, preferred_element_type=jnp.float32
        )
        inner_sum = jnp.sum(probability * weight_adjoint, axis=(1, 2), keepdims=True)
        score_adjoint = (probability * (weight_adjoint - inner_sum) * scale_factor).astype(
            jnp.bfloat16
        )
        query_adjoints.append(
            jnp.einsum(
                "rks,kse->re", score_adjoint, key_head, preferred_element_type=jnp.float32
            ).astype(jnp.bfloat16)
        )
        key_partials.append(
            jnp.einsum(
                "rks,re->kse", score_adjoint, query_head, preferred_element_type=jnp.float32
            ).astype(jnp.bfloat16)
        )
        value_partials.append(
            jnp.einsum(
                "rks,re->kse", rounded_prob, adjoint_head, preferred_element_type=jnp.float32
            ).astype(jnp.bfloat16)
        )
    attended = jnp.concatenate(attended_parts, axis=1)
    queries_adjoint = jnp.concatenate(query_adjoints, axis=1)
    partials = jnp.stack(
        [jnp.concatenate(key_partials, axis=2), jnp.concatenate(value_partials, axis=2)], axis=1
    )
    collected = partials[0].astype(jnp.float32)
    for lag_index in range(1, WIN + 1):
        collected = collected + passed_along(partials[lag_index], "ctx", -lag_index).astype(
            jnp.float32
        )
    keys_adjoint = collected[0].astype(jnp.bfloat16)
    values_adjoint = collected[1].astype(jnp.bfloat16)
    signal = attended.astype(jnp.float32)
    blocks_signal = signal.reshape(pieces, piece_rows, channels)
    end_weights = jnp.exp(-decay_rates[None] * (piece_rows - 1.0 - offsets))
    piece_ends = jnp.einsum(
        "qpc,mqc->mpc", end_weights, blocks_signal, precision=lax.Precision.HIGHEST
    )
    tail_state = jnp.sum(
        jnp.exp(-decay_rates[None] * ((pieces - 1.0 - piece_index) * piece_rows)) * piece_ends,
        axis=0,
    )

    def forward_turn(turn_index, moving):
        return passed_along(device_decay * moving + tail_state, "ctx", 1)

    arriving = lax.fori_loop(0, members, forward_turn, jnp.zeros_like(tail_state)) / loop_gap
    entering = jnp.exp(-decay_rates[None] * (offsets + 1.0))

    def forward_step(carried, step_item):
        segment, matched = step_item
        local_part = start_weights * jnp.cumsum(growth * segment[:, None, :], axis=0)
        states = local_part + entering * carried[None]
        mixture = jnp.sum(mixing[None] * states, axis=1) + skip_gain[None] * segment
        product = jnp.sum(weights[None] * matched[:, None, :] * states, axis=0)
        return (states[-1], (mixture, product))

    closing, (mixed_rows, products) = lax.scan(
        forward_step, arriving, (blocks_signal, blocks_delta)
    )
    gate_adjoint = (cotangent.astype(jnp.float32) * mixed_rows.reshape(tok_rows, channels)).astype(
        jnp.bfloat16
    )
    residues_adjoint = lax.psum(jnp.sum(products, axis=0), "ctx")
    return (queries_adjoint, keys_adjoint, values_adjoint, gate_adjoint, residues_adjoint)


def solution(mesh):
    in_specs = (
        P(("dp", "ctx"), "head"),
        P(("dp", "ctx"), "head"),
        P(("dp", "ctx"), "head"),
        P(("dp", "ctx"), "head"),
        P(("dp", "ctx"), "head"),
        P(None, "head"),
        P(None, "head"),
        P("head"),
    )
    out_specs = (
        P(("dp", "ctx"), "head"),
        P(("dp", "ctx"), "head"),
        P(("dp", "ctx"), "head"),
        P(("dp", "ctx"), "head"),
        P("dp", "head"),
    )
    members = mesh.shape["ctx"]

    def chosen(*arrays):
        rows, channels = arrays[0].shape
        whole = members == WIN and rows % 128 == 0 and (channels // HEAD) % members == 0
        return (fast_local if whole and arrays[5].shape[0] % POLE_GROUP == 0 else local)(*arrays)

    return jax.shard_map(chosen, mesh=mesh, in_specs=in_specs, out_specs=out_specs, check_vma=False)
```

```python
import functools
import math

import jax
import jax.numpy as jnp
from jax import lax
from jax.experimental import pallas as pl
from jax.experimental.pallas import tpu as pltpu
from jax.sharding import PartitionSpec as P

HEAD = 128
WIN = 4
SEGS = 8
POLE_GROUP = 8
AHEAD = 2
MESH = pl.DeviceIdType.MESH


def decay_gap(x):
    inner = 1.0 - x * (1.0 / 7.0)
    for order in (6.0, 5.0, 4.0, 3.0, 2.0):
        inner = 1.0 - x * (1.0 / order) * inner
    return x * inner


def row_of(ref, kind, pole):
    return jnp.broadcast_to(ref[kind, pl.ds(pole, 1), :], (SEGS, HEAD))


def periodic_start(ends, par_ref, pole, backward):
    total = ends
    for power, kind in ((1, 3), (2, 4), (4, 5)):
        shift = SEGS - power if backward else power
        total = total + row_of(par_ref, kind, pole) * pltpu.roll(total, shift, 0)
    total = total * row_of(par_ref, 6, pole)
    return pltpu.roll(total, SEGS - 1 if backward else 1, 0)


def segment_ends(x_ref, par_ref, poles, steps, backward, unroll=4):
    lams = [row_of(par_ref, 0, pole) for pole in range(poles)]

    def body(index, states):
        for sub in range(unroll):
            step = index * unroll + sub
            if backward:
                step = steps - 1 - step
            x = x_ref[pl.ds(step, SEGS, stride=steps + 1), :]
            states = tuple(lam * state + x for lam, state in zip(lams, states))
        return states

    zeros = tuple(jnp.zeros((SEGS, HEAD), jnp.float32) for _ in range(poles))
    ends = lax.fori_loop(0, steps // unroll, body, zeros)
    return [periodic_start(end, par_ref, pole, backward) for pole, end in enumerate(ends)]


def tree_sum(terms):
    terms = list(terms)
    while len(terms) > 1:
        paired = [a + b for a, b in zip(terms[::2], terms[1::2])]
        if len(terms) % 2:
            paired.append(terms[-1])
        terms = paired
    return terms[0]


def fast_kernel(
    members, local_heads,
    q_ref, k_ref, v_ref, gate_ref, cot_ref, decay_ref, residue_ref, skip_ref,
    dq_ref, dk_ref, dv_ref, dgate_ref, dres_ref,
    stage, inbox, outbox, landed, res_box, res_landed, res_wide,
    cot_v, gate_v, decay_v, residue_v, skip_v, par_ref, delta_ref, y_ref, att_ref, da_ref, dk_acc, dv_acc,
    in_send, in_recv, grad_send, grad_recv, mix_send, mix_recv, res_send, res_recv,
    load_sem, stage_sem, out_sem,
):
    me = lax.axis_index("ctx")
    rows = q_ref.shape[0]
    tokens = rows * members
    steps = tokens // SEGS
    poles = decay_v.shape[0]
    group = local_heads // members
    scale = 1.0 / math.sqrt(HEAD)

    barrier = pltpu.get_barrier_semaphore()
    for off in range(1, members):
        pl.semaphore_signal(
            barrier, inc=1, device_id={"ctx": lax.rem(me + off, members)}, device_id_type=MESH
        )
    owned = pl.ds(pl.multiple_of(me * (group * HEAD), HEAD), group * HEAD)
    loads = [
        pltpu.make_async_copy(src, dst, load_sem.at[index])
        for index, (src, dst) in enumerate((
            (cot_ref, cot_v), (gate_ref, gate_v), (decay_ref.at[:, owned], decay_v),
            (residue_ref.at[:, owned], residue_v), (skip_ref.at[:, owned], skip_v),
        ))
    ]
    for load in loads[:2]:
        load.start()

    def lanes(owner, head):
        return pl.ds(pl.multiple_of((owner * group + head) * HEAD, HEAD), HEAD)

    def stage_copy(head, owner, kind):
        return pltpu.make_async_copy(
            (q_ref, k_ref, v_ref)[kind].at[:, lanes(owner, head)],
            stage.at[head, owner, kind + 1], stage_sem.at[head, owner, kind],
        )

    def start_stage(head, carry):
        for kind in range(3):
            stage_copy(head, me, kind).start()
        return carry

    pl.semaphore_wait(barrier, members - 1)

    def rows_of(owner):
        return pl.ds(pl.multiple_of(owner * rows, rows), rows)

    def dest(off):
        return lax.rem(me + off, members)

    def source(off):
        return lax.rem(me + members - off, members)

    def remote(src, dst, send, recv, target):
        return pltpu.make_async_remote_copy(
            src_ref=src, dst_ref=dst, send_sem=send, recv_sem=recv,
            device_id={"ctx": target}, device_id_type=MESH,
        )

    def in_copy(head, off, kind, owner):
        if kind == 0:
            src = stage.at[head, dest(off), 0]
        else:
            src = (q_ref, k_ref, v_ref)[kind - 1].at[:, lanes(dest(off), head)]
        return remote(
            src, inbox.at[head, kind, rows_of(owner), :],
            in_send.at[head, off - 1, kind], in_recv.at[head, off - 1, kind], dest(off),
        )

    def grad_copy(head, off, owner):
        return remote(
            outbox.at[head, pl.ds(0, 3), rows_of(dest(off)), :],
            landed.at[head, owner, pl.ds(0, 3)],
            grad_send.at[head, off - 1], grad_recv.at[head, off - 1], dest(off),
        )

    def mix_copy(head, off, owner):
        return remote(
            outbox.at[head, pl.ds(3, 1), rows_of(dest(off)), :],
            landed.at[head, owner, pl.ds(3, 1)],
            mix_send.at[head, off - 1], mix_recv.at[head, off - 1], dest(off),
        )

    def res_copy(head, off, owner):
        return remote(
            res_box.at[head], res_landed.at[head, owner],
            res_send.at[head, off - 1], res_recv.at[head, off - 1], dest(off),
        )

    odd = lax.rem(me, 2)
    far_first = (2, 3 - 2 * odd, 1 + 2 * odd) if members == 4 else tuple(range(1, members))

    def send_rows(head, carry):
        for kind in range(1, 4):
            for off in far_first:
                in_copy(head, off, kind, me).start()
        return carry

    def send_delta(head, carry):
        for owner in range(members):
            here = lanes(owner, head)
            stage[head, owner, 0] = (
                cot_v[:, here].astype(jnp.float32) * gate_v[:, here].astype(jnp.float32)
            ).astype(jnp.bfloat16)
        for off in far_first:
            in_copy(head, off, 0, me).start()
        return carry

    send_rows(0, 0)
    lax.fori_loop(0, group, start_stage, 0)
    for load in loads[2:]:
        load.start()
    for load in loads[:2]:
        load.wait()
    send_delta(0, 0)
    for head in range(1, min(AHEAD, group)):
        send_rows(head, 0)
        send_delta(head, 0)
    for load in loads[2:]:
        load.wait()

    def one_head(head, carry):
        mine = pl.ds(pl.multiple_of(head * HEAD, HEAD), HEAD)
        damping = decay_v[:, mine]
        weights = jnp.sqrt(decay_gap(2.0 * damping))
        par_ref[0] = 1.0 - decay_gap(damping)
        par_ref[1] = residue_v[:, mine] * weights
        par_ref[2] = weights
        par_ref[3] = jnp.exp(-damping * steps)
        par_ref[4] = jnp.exp(-damping * (2 * steps))
        par_ref[5] = jnp.exp(-damping * (4 * steps))
        par_ref[6] = 1.0 / (1.0 - jnp.exp(-damping * tokens))
        skip = jnp.broadcast_to(skip_v[:, mine], (SEGS, HEAD))
        for kind in range(3):
            stage_copy(head, me, kind).wait()
        inbox[head, :, rows_of(me), :] = stage[head, me]
        for off in range(1, members):
            for kind in range(4):
                in_copy(head, off, kind, source(off)).wait_recv()

        @pl.when(head + AHEAD < group)
        def _():
            send_rows(head + AHEAD, 0)
            send_delta(head + AHEAD, 0)

        for seg in range(SEGS):
            delta_ref[pl.ds(seg * (steps + 1), steps), :] = inbox[
                head, 0, pl.ds(seg * steps, steps), :
            ].astype(jnp.float32)

        entering = segment_ends(delta_ref, par_ref, poles, steps, True)
        lams = [row_of(par_ref, 0, pole) for pole in range(poles)]
        mixes = [row_of(par_ref, 1, pole) for pole in range(poles)]

        def backward_body(index, states):
            for sub in range(2):
                step = steps - 1 - (index * 2 + sub)
                x = delta_ref[pl.ds(step, SEGS, stride=steps + 1), :]
                states = tuple(lam * state + x for lam, state in zip(lams, states))
                y_ref[pl.ds(step, SEGS, stride=steps + 1), :] = skip * x + tree_sum(
                    mix * state for mix, state in zip(mixes, states)
                )
            return states

        lax.fori_loop(0, steps // 2, backward_body, tuple(entering))
        for seg in range(SEGS):
            da_ref[pl.ds(seg * steps, steps), :] = y_ref[
                pl.ds(seg * (steps + 1), steps), :
            ].astype(jnp.bfloat16)

        key_head = inbox[head, 2]
        value_head = inbox[head, 3]
        for block in range(members):
            span = pl.ds(block * rows, rows)
            query = inbox[head, 1, span, :]
            adjoint = da_ref[span, :]
            scores = lax.dot_general(
                query, key_head, (((1,), (1,)), ((), ())), preferred_element_type=jnp.float32
            ) * scale
            raised = jnp.exp(scores - jnp.max(scores, axis=1, keepdims=True))
            probability = raised * (1.0 / jnp.sum(raised, axis=1, keepdims=True))
            rounded = probability.astype(jnp.bfloat16)
            attended = jnp.dot(rounded, value_head, preferred_element_type=jnp.float32)
            attended = attended.astype(jnp.bfloat16).astype(jnp.float32)
            for part in range(rows // steps):
                seg = block * (rows // steps) + part
                att_ref[pl.ds(seg * (steps + 1), steps), :] = attended[
                    part * steps : (part + 1) * steps
                ]
            weight_adjoint = lax.dot_general(
                adjoint, value_head, (((1,), (1,)), ((), ())), preferred_element_type=jnp.float32
            )
            inner = jnp.sum(probability * weight_adjoint, axis=1, keepdims=True)
            score_adjoint = (probability * (weight_adjoint - inner) * scale).astype(jnp.bfloat16)
            outbox[head, 0, span, :] = jnp.dot(
                score_adjoint, key_head, preferred_element_type=jnp.float32
            ).astype(jnp.bfloat16)
            key_part = lax.dot_general(
                score_adjoint, query, (((0,), (0,)), ((), ())), preferred_element_type=jnp.float32
            )
            value_part = lax.dot_general(
                rounded, adjoint, (((0,), (0,)), ((), ())), preferred_element_type=jnp.float32
            )
            if block == 0:
                dk_acc[...] = key_part
                dv_acc[...] = value_part
            else:
                dk_acc[...] += key_part
                dv_acc[...] += value_part
        outbox[head, 1] = dk_acc[...].astype(jnp.bfloat16)
        outbox[head, 2] = dv_acc[...].astype(jnp.bfloat16)
        for off in far_first:
            grad_copy(head, off, me).start()

        entering_forward = segment_ends(att_ref, par_ref, poles, steps, False)
        for first in range(0, poles, POLE_GROUP):
            chosen = range(first, first + POLE_GROUP)
            group_lams = [row_of(par_ref, 0, pole) for pole in chosen]
            group_mixes = [row_of(par_ref, 1, pole) for pole in chosen]

            def forward_body(index, item, first=first, lams=group_lams, mixes=group_mixes):
                states, sums = item
                for sub in range(2):
                    step = index * 2 + sub
                    here = pl.ds(step, SEGS, stride=steps + 1)
                    x = att_ref[here, :]
                    delta = delta_ref[here, :]
                    states = tuple(lam * state + x for lam, state in zip(lams, states))
                    sums = tuple(total + delta * state for total, state in zip(sums, states))
                    base = skip * x if first == 0 else y_ref[here, :]
                    y_ref[here, :] = base + tree_sum(
                        mix * state for mix, state in zip(mixes, states)
                    )
                return states, sums

            zeros = tuple(jnp.zeros((SEGS, HEAD), jnp.float32) for _ in chosen)
            starts = tuple(entering_forward[pole] for pole in chosen)
            unused, sums = lax.fori_loop(0, steps // 2, forward_body, (starts, zeros))
            for pole, total in zip(chosen, sums):
                par_ref[7, pl.ds(pole, 1), :] = (
                    jnp.sum(total, axis=0, keepdims=True) * par_ref[2, pl.ds(pole, 1), :]
                )
        res_box[head] = par_ref[7].astype(jnp.bfloat16)
        for seg in range(SEGS):
            outbox[head, 3, pl.ds(seg * steps, steps), :] = y_ref[
                pl.ds(seg * (steps + 1), steps), :
            ].astype(jnp.bfloat16)
        for off in far_first:
            mix_copy(head, off, me).start()
            res_copy(head, off, me).start()
        landed[head, me] = outbox[head, :, rows_of(me), :]
        res_landed[head, me] = res_box[head]
        return carry

    lax.fori_loop(0, group, one_head, 0)

    def out_copy(head, owner, kind):
        src = res_wide.at[head, owner] if kind == 4 else landed.at[head, owner, kind]
        target = (dq_ref, dk_ref, dv_ref, dgate_ref, dres_ref)[kind]
        return pltpu.make_async_copy(
            src, target.at[:, lanes(owner, head)], out_sem.at[head, owner, kind]
        )

    def finish(head, carry):
        for off in range(1, members):
            grad_copy(head, off, source(off)).wait_recv()
        for owner in range(members):
            for kind in range(3):
                out_copy(head, owner, kind).start()
        for off in range(1, members):
            mix_copy(head, off, source(off)).wait_recv()
            res_copy(head, off, source(off)).wait_recv()
        for owner in range(members):
            landed[head, owner, 3] = (
                cot_v[:, lanes(owner, head)].astype(jnp.float32)
                * landed[head, owner, 3].astype(jnp.float32)
            ).astype(jnp.bfloat16)
            res_wide[head, owner] = res_landed[head, owner].astype(jnp.float32)
            for kind in range(3, 5):
                out_copy(head, owner, kind).start()
        return carry

    lax.fori_loop(0, group, finish, 0)
    def sent(head, carry):
        for off in range(1, members):
            for kind in range(4):
                in_copy(head, off, kind, me).wait_send()
            grad_copy(head, off, me).wait_send()
            mix_copy(head, off, me).wait_send()
            res_copy(head, off, me).wait_send()
        for owner in range(members):
            for kind in range(5):
                out_copy(head, owner, kind).wait()
        return carry

    lax.fori_loop(0, group, sent, 0)


def write_kernel(*refs):
    sources, targets, held, in_sem, out_sem = refs[:5], refs[5:10], refs[10:15], refs[15], refs[16]
    loads, stores = [], []
    for src, dst, middle in zip(sources, targets, held):
        width = src.shape[1] // 2
        for half in range(2):
            part = pl.ds(half * width, width)
            index = len(loads)
            loads.append(
                pltpu.make_async_copy(src.at[:, part], middle.at[:, part], in_sem.at[index])
            )
            stores.append(
                pltpu.make_async_copy(middle.at[:, part], dst.at[:, part], out_sem.at[index])
            )
    for load in loads:
        load.start()
    for load, store in zip(loads, stores):
        load.wait()
        store.start()
    for store in stores:
        store.wait()


def fast_local(queries, key_rows, value_rows, gate_values, cotangent, decay_rates, residues, skip_gain):
    members = lax.axis_size("ctx")
    rows, channels = queries.shape
    local_heads = channels // HEAD
    group = local_heads // members
    tokens = rows * members
    poles = decay_rates.shape[0]
    wide = jax.ShapeDtypeStruct((rows, channels), jnp.bfloat16)
    sems = pltpu.SemaphoreType.DMA((group, members - 1))
    hbm = pl.BlockSpec(memory_space=pltpu.HBM)
    shapes = (wide, wide, wide, wide, jax.ShapeDtypeStruct((poles, channels), jnp.float32))
    results = pl.pallas_call(
        functools.partial(fast_kernel, members, local_heads),
        out_shape=shapes,
        in_specs=[hbm] * 8,
        out_specs=(hbm,) * 5,
        scratch_shapes=[
            pltpu.VMEM((group, members, 4, rows, HEAD), jnp.bfloat16),
            pltpu.VMEM((group, 4, tokens, HEAD), jnp.bfloat16),
            pltpu.VMEM((group, 4, tokens, HEAD), jnp.bfloat16),
            pltpu.VMEM((group, members, 4, rows, HEAD), jnp.bfloat16),
            pltpu.VMEM((group, poles, HEAD), jnp.bfloat16),
            pltpu.VMEM((group, members, poles, HEAD), jnp.bfloat16),
            pltpu.VMEM((group, members, poles, HEAD), jnp.float32),
            pltpu.VMEM((rows, channels), jnp.bfloat16),
            pltpu.VMEM((rows, channels), jnp.bfloat16),
            pltpu.VMEM((poles, group * HEAD), jnp.float32),
            pltpu.VMEM((poles, group * HEAD), jnp.float32),
            pltpu.VMEM((1, group * HEAD), jnp.float32),
            pltpu.VMEM((8, poles, HEAD), jnp.float32),
            pltpu.VMEM((tokens + SEGS, HEAD), jnp.float32),
            pltpu.VMEM((tokens + SEGS, HEAD), jnp.float32),
            pltpu.VMEM((tokens + SEGS, HEAD), jnp.float32),
            pltpu.VMEM((tokens, HEAD), jnp.bfloat16),
            pltpu.VMEM((tokens, HEAD), jnp.float32),
            pltpu.VMEM((tokens, HEAD), jnp.float32),
        ] + [pltpu.SemaphoreType.DMA((group, members - 1, 4))] * 2 + [sems] * 6 + [
            pltpu.SemaphoreType.DMA((5,)), pltpu.SemaphoreType.DMA((group, members, 3)),
            pltpu.SemaphoreType.DMA((group, members, 5)),
        ],
        compiler_params=pltpu.CompilerParams(
            collective_id=0, has_side_effects=True, vmem_limit_bytes=60 * 1024 * 1024
        ),
    )(queries, key_rows, value_rows, gate_values, cotangent, decay_rates, residues,
      skip_gain.reshape(1, channels))
    return pl.pallas_call(
        write_kernel,
        out_shape=shapes,
        in_specs=[hbm] * 5,
        out_specs=(hbm,) * 5,
        scratch_shapes=[pltpu.VMEM(shape.shape, shape.dtype) for shape in shapes]
        + [pltpu.SemaphoreType.DMA((10,))] * 2,
        compiler_params=pltpu.CompilerParams(vmem_limit_bytes=60 * 1024 * 1024),
    )(*results)


def passed_along(array, axis, by):
    length = lax.axis_size(axis)
    return lax.ppermute(array, axis, [(i, (i + by) % length) for i in range(length)])


def window_mask(row_count):
    row_ids = jnp.arange(row_count)[:, None, None]
    lag_ids = jnp.arange(WIN + 1)[None, :, None]
    column_ids = jnp.arange(row_count)[None, None, :]
    return ((lag_ids > 0) | (column_ids <= row_ids)) & ((lag_ids < WIN) | (column_ids > row_ids))


def local(queries, key_rows, value_rows, gate_values, cotangent, decay_rates, residues, skip_gain):
    members = lax.axis_size("ctx")
    tok_rows, channels = queries.shape
    local_heads = channels // HEAD
    scale_factor = 1.0 / math.sqrt(HEAD)
    weights = jnp.sqrt(-jnp.expm1(-2.0 * decay_rates))
    mixing = residues * weights
    loop_gap = -jnp.expm1(-decay_rates * (tok_rows * members))
    device_decay = jnp.exp(-decay_rates * tok_rows)
    piece_rows = min(128, tok_rows)
    pieces = tok_rows // piece_rows
    offsets = jnp.arange(piece_rows, dtype=jnp.float32)[:, None, None]
    piece_index = jnp.arange(pieces, dtype=jnp.float32)[:, None, None]
    start_weights = jnp.exp(-decay_rates[None] * offsets)
    growth = jnp.exp(decay_rates[None] * offsets)
    delta_rows = cotangent.astype(jnp.float32) * gate_values.astype(jnp.float32)
    blocks_delta = delta_rows.reshape(pieces, piece_rows, channels)
    piece_starts = jnp.einsum(
        "qpc,mqc->mpc", start_weights, blocks_delta, precision=lax.Precision.HIGHEST
    )
    head_state = jnp.sum(
        jnp.exp(-decay_rates[None] * (piece_index * piece_rows)) * piece_starts, axis=0
    )

    def backward_turn(turn_index, moving):
        return passed_along(device_decay * moving + head_state, "ctx", -1)

    incoming = lax.fori_loop(0, members, backward_turn, jnp.zeros_like(head_state)) / loop_gap

    def backward_step(carried, segment):
        local_part = growth * lax.cumsum(start_weights * segment[:, None, :], axis=0, reverse=True)
        states = local_part + jnp.exp(-decay_rates[None] * (piece_rows - offsets)) * carried[None]
        mixture = jnp.sum(mixing[None] * states, axis=1) + skip_gain[None] * segment
        return (states[0], mixture)

    unused_state, adjoint_rows = lax.scan(backward_step, incoming, blocks_delta, reverse=True)
    attended_adjoint = adjoint_rows.reshape(tok_rows, channels).astype(jnp.bfloat16)
    key_value = jnp.stack([key_rows, value_rows])
    window = [key_value]
    moving = key_value
    for lag_index in range(WIN):
        moving = passed_along(moving, "ctx", 1)
        window.append(moving)
    stacked = jnp.stack(window)
    key_window = stacked[:, 0]
    value_window = stacked[:, 1]
    allowed = window_mask(tok_rows)
    attended_parts = []
    query_adjoints = []
    key_partials = []
    value_partials = []
    for head_index in range(local_heads):
        first = head_index * HEAD
        query_head = queries[:, first : first + HEAD]
        key_head = key_window[:, :, first : first + HEAD]
        value_head = value_window[:, :, first : first + HEAD]
        adjoint_head = attended_adjoint[:, first : first + HEAD]
        scores = (
            jnp.einsum("re,kse->rks", query_head, key_head, preferred_element_type=jnp.float32)
            * scale_factor
        )
        masked = jnp.where(allowed, scores, -jnp.inf)
        row_top = jnp.max(masked, axis=(1, 2), keepdims=True)
        raised = jnp.exp(masked - row_top)
        probability = raised / jnp.sum(raised, axis=(1, 2), keepdims=True)
        rounded_prob = probability.astype(jnp.bfloat16)
        attended_parts.append(
            jnp.einsum(
                "rks,kse->re", rounded_prob, value_head, preferred_element_type=jnp.float32
            ).astype(jnp.bfloat16)
        )
        weight_adjoint = jnp.einsum(
            "re,kse->rks", adjoint_head, value_head, preferred_element_type=jnp.float32
        )
        inner_sum = jnp.sum(probability * weight_adjoint, axis=(1, 2), keepdims=True)
        score_adjoint = (probability * (weight_adjoint - inner_sum) * scale_factor).astype(
            jnp.bfloat16
        )
        query_adjoints.append(
            jnp.einsum(
                "rks,kse->re", score_adjoint, key_head, preferred_element_type=jnp.float32
            ).astype(jnp.bfloat16)
        )
        key_partials.append(
            jnp.einsum(
                "rks,re->kse", score_adjoint, query_head, preferred_element_type=jnp.float32
            ).astype(jnp.bfloat16)
        )
        value_partials.append(
            jnp.einsum(
                "rks,re->kse", rounded_prob, adjoint_head, preferred_element_type=jnp.float32
            ).astype(jnp.bfloat16)
        )
    attended = jnp.concatenate(attended_parts, axis=1)
    queries_adjoint = jnp.concatenate(query_adjoints, axis=1)
    partials = jnp.stack(
        [jnp.concatenate(key_partials, axis=2), jnp.concatenate(value_partials, axis=2)], axis=1
    )
    collected = partials[0].astype(jnp.float32)
    for lag_index in range(1, WIN + 1):
        collected = collected + passed_along(partials[lag_index], "ctx", -lag_index).astype(
            jnp.float32
        )
    keys_adjoint = collected[0].astype(jnp.bfloat16)
    values_adjoint = collected[1].astype(jnp.bfloat16)
    signal = attended.astype(jnp.float32)
    blocks_signal = signal.reshape(pieces, piece_rows, channels)
    end_weights = jnp.exp(-decay_rates[None] * (piece_rows - 1.0 - offsets))
    piece_ends = jnp.einsum(
        "qpc,mqc->mpc", end_weights, blocks_signal, precision=lax.Precision.HIGHEST
    )
    tail_state = jnp.sum(
        jnp.exp(-decay_rates[None] * ((pieces - 1.0 - piece_index) * piece_rows)) * piece_ends,
        axis=0,
    )

    def forward_turn(turn_index, moving):
        return passed_along(device_decay * moving + tail_state, "ctx", 1)

    arriving = lax.fori_loop(0, members, forward_turn, jnp.zeros_like(tail_state)) / loop_gap
    entering = jnp.exp(-decay_rates[None] * (offsets + 1.0))

    def forward_step(carried, step_item):
        segment, matched = step_item
        local_part = start_weights * jnp.cumsum(growth * segment[:, None, :], axis=0)
        states = local_part + entering * carried[None]
        mixture = jnp.sum(mixing[None] * states, axis=1) + skip_gain[None] * segment
        product = jnp.sum(weights[None] * matched[:, None, :] * states, axis=0)
        return (states[-1], (mixture, product))

    closing, (mixed_rows, products) = lax.scan(
        forward_step, arriving, (blocks_signal, blocks_delta)
    )
    gate_adjoint = (cotangent.astype(jnp.float32) * mixed_rows.reshape(tok_rows, channels)).astype(
        jnp.bfloat16
    )
    residues_adjoint = lax.psum(jnp.sum(products, axis=0), "ctx")
    return (queries_adjoint, keys_adjoint, values_adjoint, gate_adjoint, residues_adjoint)


def solution(mesh):
    in_specs = (
        P(("dp", "ctx"), "head"),
        P(("dp", "ctx"), "head"),
        P(("dp", "ctx"), "head"),
        P(("dp", "ctx"), "head"),
        P(("dp", "ctx"), "head"),
        P(None, "head"),
        P(None, "head"),
        P("head"),
    )
    out_specs = (
        P(("dp", "ctx"), "head"),
        P(("dp", "ctx"), "head"),
        P(("dp", "ctx"), "head"),
        P(("dp", "ctx"), "head"),
        P("dp", "head"),
    )
    members = mesh.shape["ctx"]

    def chosen(*arrays):
        rows, channels = arrays[0].shape
        whole = members == WIN and rows % 128 == 0 and (channels // HEAD) % members == 0
        return (fast_local if whole and arrays[5].shape[0] % POLE_GROUP == 0 else local)(*arrays)

    return jax.shard_map(chosen, mesh=mesh, in_specs=in_specs, out_specs=out_specs, check_vma=False)
```
